256 devices in a mesh: probe: 2 (over x_hi), gx: 16 (over z, core), gy: 8 (over y, x_lo).
Axes of the slice: x: 4 (x_hi: 2, x_lo: 2; x = x_hi * 2 + x_lo), y: 4, z: 8, core: 2. Of those that a mesh axis runs over, the one named last changes fastest.
Arguments:
- probes: float32 [8, 1024, 1024], P('probe', 'gx', 'gy'), may hold values from -6 to 6
- base_velocity: float32 [2, 1024, 1024], P(None, 'gx', 'gy'), may hold values from -6 to 6
- viscosity: float32 [1024, 1024], P('gx', 'gy'), may hold values from 0.1 to 0.4
- friction: float32 [1024, 1024], P('gx', 'gy'), may hold values from 0.25 to 1
- noise_weight: float32 [1024, 1024], P('gx', 'gy'), may hold values from 1 to 16
- ice_mask: int32 [1024, 1024], P('gx', 'gy'), may hold values 0 or 1
Outputs:
- images: float32 [8, 1024, 1024], P('probe', 'gx', 'gy')
- factor: float32 [8, 1024, 1024], P('probe', 'gx', 'gy')
- gram: float32 [8, 8], replicated
The draws below stay inside these ranges and needn't reach their ends.
All inputs are finite; a program needn't handle non-finite values. No bound on the sum of `ice_mask` on one device may be relied on, other than what follows from the above.
Results may differ from the reference program's by a relative error of at most 0.000082.
Values sent between devices are 32-bit elements; how exact they have to be, the bound alone decides.
A program may use at most 64 MiB of HBM per device.

```python
import math
import jax
import jax.numpy as jnp
from jax import lax

SWEEPS = 9
PROBES = 8
NX = 1024
NY = 1024


def with_ends(array, own_key, least, largest):
    index_at = [jax.random.randint(jax.random.fold_in(own_key, axis), (), 0, length) for axis, length in enumerate(array.shape)]
    widest = array.shape.index(max(array.shape))
    next_to = index_at[:widest] + [(index_at[widest] + 1) % array.shape[widest]] + index_at[widest + 1:]
    return array.at[tuple(index_at)].set(least).at[tuple(next_to)].set(largest)


def steps_of(stream_key, extent, shards, low, largest):
    gain = 1.0
    for dim, parts in shards:
        steps = jax.random.uniform(jax.random.fold_in(jax.random.fold_in(stream_key, 6), dim), (parts,), jnp.float32, low / len(shards), largest / len(shards))
        gain = gain * jnp.repeat(jnp.exp(steps), extent[dim] // parts).reshape((-1,) + (1,) * (len(extent) - 1 - dim))
    return gain


def gaussian(key, extent, scale, reach, pieces=(), held_as=jnp.bfloat16):
    result = jax.random.normal(key, extent, jnp.float32) * scale
    if len(pieces) > 0:
        result = steps_of(key, extent, pieces, -0.22, 0.18) * result
    return jnp.clip(result, min=-reach, max=reach).astype(held_as)


def setup_inputs(seed: int = 0) -> dict:
    key_list = jax.random.split(jax.random.key(seed), 7)
    return {
        "probes": gaussian(key_list[0], (PROBES, NX, NY), 1.0, 6.0, ((0, 2), (1, 16), (2, 8)), jnp.float32),
        "base_velocity": gaussian(key_list[1], (2, NX, NY), 1.0, 6.0, ((1, 16), (2, 8)), jnp.float32),
        "viscosity": jnp.clip(jnp.exp(math.log(0.4) - 1.3862944 * jax.random.uniform(key_list[2], (NX, NY), jnp.float32) ** steps_of(key_list[2], (NX, NY), ((0, 16), (1, 8)), -0.2, 0.2)), 0.1, 0.4),
        "friction": jnp.clip(jnp.exp(math.log(1.0) - 1.3862944 * jax.random.uniform(key_list[3], (NX, NY), jnp.float32) ** steps_of(key_list[3], (NX, NY), ((0, 16), (1, 8)), -0.2, 0.2)), 0.25, 1.0),
        "noise_weight": jnp.clip(jnp.exp(math.log(16.0) - 2.7725887 * jax.random.uniform(key_list[4], (NX, NY), jnp.float32) ** steps_of(key_list[4], (NX, NY), ((0, 16), (1, 8)), -0.2, 0.2)), 1.0, 16.0),
        "ice_mask": with_ends((jax.random.randint(key_list[5], (NX, NY), 0, 4) < 3).astype(jnp.int32), jax.random.fold_in(key_list[5], 1), 0, 1),
    }


OMEGA = 0.6
DRAG = 0.05
PRIOR = 0.05

def near(values, step_x, step_y):
    row_count = values.shape[-2]
    column_count = values.shape[-1]
    return values[..., 1 + step_x:row_count - 1 + step_x, 1 + step_y:column_count - 1 + step_y]

def diagonal_of(eta_pad, react):
    eta_mid = near(eta_pad, 0, 0)
    sum_first = near(eta_pad, 1, 0) + near(eta_pad, -1, 0)
    sum_second = near(eta_pad, 0, 1) + near(eta_pad, 0, -1)
    first = 2.0 * (2.0 * eta_mid + sum_first) + 0.5 * (2.0 * eta_mid + sum_second) + react
    second = 0.5 * (2.0 * eta_mid + sum_first) + 2.0 * (2.0 * eta_mid + sum_second) + react
    return jnp.stack([first, second], axis=-3)

def stencil(field_pad, eta_pad, react):
    eta_mid = near(eta_pad, 0, 0)
    eta_east = near(eta_pad, 1, 0)
    eta_west = near(eta_pad, -1, 0)
    eta_north = near(eta_pad, 0, 1)
    eta_south = near(eta_pad, 0, -1)
    along_x = field_pad[..., 0, :, :]
    along_y = field_pad[..., 1, :, :]
    x_mid = near(along_x, 0, 0)
    x_east = near(along_x, 1, 0)
    x_west = near(along_x, -1, 0)
    x_north = near(along_x, 0, 1)
    x_south = near(along_x, 0, -1)
    x_northeast = near(along_x, 1, 1)
    x_southeast = near(along_x, 1, -1)
    x_northwest = near(along_x, -1, 1)
    x_southwest = near(along_x, -1, -1)
    y_mid = near(along_y, 0, 0)
    y_east = near(along_y, 1, 0)
    y_west = near(along_y, -1, 0)
    y_north = near(along_y, 0, 1)
    y_south = near(along_y, 0, -1)
    y_northeast = near(along_y, 1, 1)
    y_southeast = near(along_y, 1, -1)
    y_northwest = near(along_y, -1, 1)
    y_southwest = near(along_y, -1, -1)
    first = 2.0 * (eta_mid + eta_east) * (x_mid - x_east) + 2.0 * (eta_mid + eta_west) * (x_mid - x_west) + 0.5 * (eta_mid + eta_north) * (x_mid - x_north) + 0.5 * (eta_mid + eta_south) * (x_mid - x_south) - 0.5 * (eta_east * (y_northeast - y_southeast) - eta_west * (y_northwest - y_southwest)) - 0.25 * (eta_north * (y_northeast - y_northwest) - eta_south * (y_southeast - y_southwest)) + react * x_mid
    second = 0.5 * (eta_mid + eta_east) * (y_mid - y_east) + 0.5 * (eta_mid + eta_west) * (y_mid - y_west) + 2.0 * (eta_mid + eta_north) * (y_mid - y_north) + 2.0 * (eta_mid + eta_south) * (y_mid - y_south) - 0.5 * (eta_north * (x_northeast - x_northwest) - eta_south * (x_southeast - x_southwest)) - 0.25 * (eta_east * (x_northeast - x_southeast) - eta_west * (x_northwest - x_southwest)) + react * y_mid
    return jnp.stack([first, second], axis=-3)

def reference(probes, base_velocity, viscosity, friction, noise_weight, ice_mask):
    ice = ice_mask.astype(jnp.float32)
    coupling = friction * ice
    react = coupling + DRAG
    eta_pad = jnp.pad(viscosity, 1)
    diag = diagonal_of(eta_pad, react)

    def relax(source):
        state = OMEGA * source / diag
        for sweep in range(SWEEPS - 1):
            padded = jnp.pad(state, ((0, 0), (1, 1), (1, 1)))
            state = state + OMEGA * (source - stencil(padded, eta_pad, react)) / diag
        return state

    def image_of(probe):
        source = -coupling * base_velocity * probe
        response = relax(source)
        adjoint = relax(noise_weight * response)
        return -coupling * jnp.sum(base_velocity * adjoint, axis=0) + PRIOR * probe
    images = lax.map(image_of, probes)
    flat_probes = probes.reshape(PROBES, -1)
    flat_images = images.reshape(PROBES, -1)
    gram = jnp.dot(flat_probes, flat_images.T, precision=lax.Precision.HIGHEST) / (NX * NY)
    lower = jnp.linalg.cholesky(gram)
    solved = jax.scipy.linalg.solve_triangular(lower, flat_images, lower=True)
    factor = solved.reshape(images.shape)
    return (images, factor, gram)
```

```python
import functools

import jax
import jax.numpy as jnp
from jax import lax
from jax.experimental import pallas as pl
from jax.experimental.pallas import tpu as pltpu
from jax.sharding import PartitionSpec as P

SWEEPS = 9
OMEGA = 0.6
DRAG = 0.05
PRIOR = 0.05

HALF = 4
ROWS, COLS = 64, 128
HALO = 2 * (SWEEPS - 1)
BI, BJ = (ROWS + 2 * HALO) // 8, (COLS + 2 * HALO) // 32
EXT = ROWS + 2 * HALO
ETA_HALO = 24
MESH = pl.DeviceIdType.MESH
F32 = jnp.float32
AROUND = ((-1, 0), (1, 0), (0, -1), (0, 1), (-1, -1), (-1, 1), (1, -1), (1, 1))


def lanes():
    return lax.broadcasted_iota(jnp.int32, (8, 128), 1)


def sublanes():
    return lax.broadcasted_iota(jnp.int32, (8, 128), 0)


def turn(x, shift, axis):
    shift = shift % x.shape[axis]
    return pltpu.roll(x, shift, axis) if shift else x


def pick(x, index):
    return jnp.take_along_axis(x, index, axis=1, mode="promise_in_bounds")


def unrolled(count, body):
    def step(i, carry):
        body(i)
        return carry

    lax.fori_loop(0, count, step, 0, unroll=True)


def pack_strips(ext, eta, left, right, eta_left, eta_right):
    lane = lax.broadcasted_iota(jnp.int32, (ROWS, COLS), 1)
    for f in range(8):
        own = ext[f, HALO : HALO + ROWS, :]
        here = (lane >= 16 * f) & (lane < 16 * f + 16)
        first, last = turn(own, 16 * f, 1), turn(own, 16 * f + 16, 1)
        left[...] = first if f == 0 else jnp.where(here, first, left[...])
        right[...] = last if f == 0 else jnp.where(here, last, right[...])
    lane = lax.broadcasted_iota(jnp.int32, (16, COLS), 1)
    first = last = None
    for g in range(4):
        own = eta[ETA_HALO + 16 * g : ETA_HALO + 16 * g + 16, :]
        here = (lane >= 32 * g) & (lane < 32 * g + 32)
        a, b = turn(own, 32 * g, 1), turn(own, 32 * g + 32, 1)
        first = a if g == 0 else jnp.where(here, a, first)
        last = b if g == 0 else jnp.where(here, b, last)
    eta_left[...] = first
    eta_right[...] = last


def relayout(ext, west, east, eta, eta_west, eta_east, side, eta_side, spread, eta_spread):
    lane = lanes()
    block = lane & 31
    group = lane >> 5
    wide = lax.broadcasted_iota(jnp.int32, (EXT, COLS), 1)
    w, e = west[...], east[...]
    side[0] = jnp.where(wide < 64, w, turn(e, 64, 1))
    side[1] = jnp.where(wide < 64, turn(w, 64, 1), e)
    for k in range(14):
        own_row = 8 * k - ETA_HALO
        slot = 0 if own_row < 0 else (1 if own_row < ROWS else 2)
        row = own_row - ROWS * (slot - 1)
        g, r = row // 16, row % 16
        a = turn(eta_west[slot, r : r + 8, :], -32 * g, 1)
        b = turn(eta_east[slot, r : r + 8, :], 32 - 32 * g, 1)
        eta_side[8 * k : 8 * k + 8, :] = jnp.where(lane < 32, a, b)

    def places(j):
        col = BJ * block + j - HALO
        own = jnp.clip(col, 0, COLS - 1)
        outside = (col < 0) | (col >= COLS)
        return col, own, outside

    def fields(i):
        rows = pl.ds(i, 8, stride=BI)
        own = [ext[f, rows, :] for f in range(8)]
        low, high = side[0, rows, :], side[1, rows, :]
        for j in range(BJ):
            col, at, outside = places(j)
            near_side = jnp.where(outside, jnp.where(col < 0, col + HALO, col - COLS + 64), 0)
            value = pick(own[HALF - 1], at)
            for p in range(HALF - 2, -1, -1):
                value = jnp.where(group == p, pick(own[p], at), value)
            spread[0, i, j] = jnp.where(outside, pick(low, near_side + 16 * group), value)
            for f in range(4):
                spread[1 + f, i, j] = jnp.where(outside, pick(high, near_side + 16 * f), pick(own[4 + f], at))

    unrolled(BI, fields)

    def viscosity(i):
        rows = pl.ds(i + ETA_HALO - HALO - 1, 8, stride=BI)
        own, beside = eta[rows, :], eta_side[rows, :]
        for j in range(-1, BJ + 1):
            col, at, outside = places(j)
            near_side = jnp.where(outside, jnp.where(col < 0, col + 32, col - COLS + 32), 0)
            eta_spread[i, j + 1] = jnp.where(outside, pick(beside, near_side), pick(own, at))

    unrolled(BI + 2, viscosity)


def store_state(state, c, i, values):
    values = [turn(values[BJ - 1], 1, 1)] + values + [turn(values[0], -1, 1)]
    for j, value in enumerate(values):
        state[c, i + 1, j] = value

    def before(i):
        for j, value in enumerate(values):
            state[c, 0, j] = turn(value, 1, 0)

    def after(i):
        for j, value in enumerate(values):
            state[c, BI + 1, j] = turn(value, -1, 0)

    return before, after


def wrap_rows(state):
    for c in range(2):
        for j in range(BJ + 2):
            state[c, 0, j] = turn(state[c, BI, j], 1, 0)
            state[c, BI + 1, j] = turn(state[c, 1, j], -1, 0)


def coefficients(spread, eta_spread, coef, weight, source, state, gx, gy, nx, ny):
    lane, sub = lanes(), sublanes()

    def row(i):
        r = gx * ROWS - HALO + BI * sub + i
        row_in = (r >= 0) & (r < nx)
        first, second = [], []
        for j in range(BJ):
            c = gy * COLS - HALO + BJ * (lane & 31) + j
            inside = row_in & (c >= 0) & (c < ny)
            m = eta_spread[i + 1, j + 1]
            e, w = eta_spread[i + 2, j + 1], eta_spread[i, j + 1]
            n, s = eta_spread[i + 1, j + 2], eta_spread[i + 1, j]
            react = spread[3, i, j] + DRAG
            me, mw, mn, ms = m + e, m + w, m + n, m + s
            along, across = me + mw, mn + ms
            w1 = jnp.where(inside, OMEGA / (2.0 * along + 0.5 * across + react), 0.0)
            w2 = jnp.where(inside, OMEGA / (0.5 * along + 2.0 * across + react), 0.0)
            a1, b1, q1 = 2.0 * w1, 0.5 * w1, 0.25 * w1
            a2, b2, q2 = 2.0 * w2, 0.5 * w2, 0.25 * w2
            coef[0, i, j] = a1 * me
            coef[1, i, j] = a1 * mw
            coef[2, i, j] = b1 * mn
            coef[3, i, j] = b1 * ms
            be, bw, qn, qs = b1 * e, b1 * w, q1 * n, q1 * s
            coef[4, i, j] = be + qn
            coef[5, i, j] = be + qs
            coef[6, i, j] = bw + qn
            coef[7, i, j] = bw + qs
            coef[8, i, j] = b2 * me
            coef[9, i, j] = b2 * mw
            coef[10, i, j] = a2 * mn
            coef[11, i, j] = a2 * ms
            bn, bs, qe, qw = b2 * n, b2 * s, q2 * e, q2 * w
            coef[12, i, j] = bn + qe
            coef[13, i, j] = bs + qe
            coef[14, i, j] = bn + qw
            coef[15, i, j] = bs + qw
            noise = spread[4, i, j]
            weight[0, i, j] = w1 * noise
            weight[1, i, j] = w2 * noise
            probe = spread[0, i, j]
            f1, f2 = w1 * (spread[1, i, j] * probe), w2 * (spread[2, i, j] * probe)
            source[0, i, j] = f1
            source[1, i, j] = f2
            first.append(f1)
            second.append(f2)
        store_state(state, 0, i, first)
        store_state(state, 1, i, second)

    unrolled(BI, row)
    wrap_rows(state)


def sweep(old, new, coef, source):
    def row(i):
        first, second = [], []
        for j in range(BJ):

            def at(c, di, dj):
                return old[c, i + 1 + di, j + 1 + dj]

            k = [coef[n, i, j] for n in range(16)]
            first.append(
                (0.4 * at(0, 0, 0) + source[0, i, j])
                + (k[0] * at(0, 1, 0) + k[1] * at(0, -1, 0))
                + (k[2] * at(0, 0, 1) + k[3] * at(0, 0, -1))
                + (k[4] * at(1, 1, 1) - k[5] * at(1, 1, -1))
                + (k[7] * at(1, -1, -1) - k[6] * at(1, -1, 1))
            )
            second.append(
                (0.4 * at(1, 0, 0) + source[1, i, j])
                + (k[8] * at(1, 1, 0) + k[9] * at(1, -1, 0))
                + (k[10] * at(1, 0, 1) + k[11] * at(1, 0, -1))
                + (k[12] * at(0, 1, 1) - k[13] * at(0, 1, -1))
                + (k[15] * at(0, -1, -1) - k[14] * at(0, -1, 1))
            )
        store_state(new, 0, i, first)
        store_state(new, 1, i, second)

    unrolled(BI, row)
    wrap_rows(new)


def relax(state_a, state_b, coef, source):
    def two(k, carry):
        sweep(state_a, state_b, coef, source)
        sweep(state_b, state_a, coef, source)
        return carry

    lax.fori_loop(0, (SWEEPS - 1) // 2, two, 0)


def next_source(state, weight, source):
    def row(i):
        for c in range(2):
            values = [weight[c, i, j] * state[c, i + 1, j + 1] for j in range(BJ)]
            for j in range(BJ):
                source[c, i, j] = values[j]
            store_state(state, c, i, values)

    unrolled(BI, row)
    wrap_rows(state)


def gather_images(state, spread, natural):
    lane = lanes()
    place = lane + HALO
    block = (place * 205) >> 10
    rest = place - BJ * block

    def row(i):
        values = [
            spread[1, i, j] * state[0, i + 1, j + 1]
            + spread[2, i, j] * state[1, i + 1, j + 1]
            + PRIOR * spread[0, i, j]
            for j in range(BJ)
        ]
        for p in range(HALF):
            out = pick(values[0], block + 32 * p)
            for j in range(1, BJ):
                out = jnp.where(rest == j, pick(values[j], block + 32 * p), out)
            natural[p, pl.ds(i, 8, stride=BI), :] = out

    unrolled(BI, row)


def products(left, left_row, right, right_row):
    def add(k, totals):
        a = [left[p, pl.ds(left_row + 8 * k, 8), :] for p in range(HALF)]
        b = [right[p, pl.ds(right_row + 8 * k, 8), :] for p in range(HALF)]
        return tuple(t + a[n // 4] * b[n % 4] for n, t in enumerate(totals))

    zero = jnp.zeros((8, 128), F32)
    totals = lax.fori_loop(0, ROWS // 8, add, (zero,) * 16, unroll=True)
    sums = jnp.concatenate([jnp.sum(t, axis=0, keepdims=True) for t in totals], axis=0)
    sums = jnp.sum(sums, axis=1, keepdims=True)
    lane = lax.broadcasted_iota(jnp.int32, (16, 128), 1)
    row = lax.broadcasted_iota(jnp.int32, (16, 128), 0)
    return jnp.sum(jnp.where(lane == row, sums, 0.0), axis=0, keepdims=True)


def main_kernel(
    nx_devices, ny_devices,
    probes, velocity, eta_in, friction, noise, ice,
    images, other_images, gram,
    ext, west, east, left, right, eta, eta_west, eta_east, eta_left, eta_right,
    vel, fric, mask, side, eta_side, spread, eta_spread, coef, weight, source, state_a, state_b,
    natural, other_probes, message, inbox_a, inbox_b,
    in_sem, halo_send, halo_recv, eta_send, eta_recv, pair_send, pair_recv,
    a_send, a_recv, b_send, b_recv,
):
    half, gx, gy = lax.axis_index("probe"), lax.axis_index("gx"), lax.axis_index("gy")
    group_a, group_b = nx_devices, 2 * ny_devices
    me_b = gy * 2 + half
    own_rows = slice(HALO, HALO + ROWS)

    loads = [
        pltpu.make_async_copy(velocity, vel, in_sem.at[0]),
        pltpu.make_async_copy(friction, fric, in_sem.at[1]),
        pltpu.make_async_copy(ice, mask, in_sem.at[2]),
        pltpu.make_async_copy(probes, ext.at[0:HALF, own_rows, :], in_sem.at[3]),
        pltpu.make_async_copy(noise, ext.at[7, own_rows, :], in_sem.at[4]),
        pltpu.make_async_copy(eta_in, eta.at[ETA_HALO : ETA_HALO + ROWS, :], in_sem.at[5]),
    ]
    for load in loads:
        load.start()

    def blank(ref):
        ref[...] = jnp.zeros(ref.shape, F32)

    @pl.when(gx == 0)
    def _():
        blank(ext.at[:, 0:HALO, :])
        blank(eta.at[0:ETA_HALO, :])
        for ref in (west, east):
            blank(ref.at[0:HALO, :])
        for ref in (eta_west, eta_east):
            blank(ref.at[0])

    @pl.when(gx == nx_devices - 1)
    def _():
        blank(ext.at[:, HALO + ROWS : EXT, :])
        blank(eta.at[ETA_HALO + ROWS : 2 * ETA_HALO + ROWS, :])
        for ref in (west, east):
            blank(ref.at[HALO + ROWS : EXT, :])
        for ref in (eta_west, eta_east):
            blank(ref.at[2])

    @pl.when(gy == 0)
    def _():
        blank(west)
        blank(eta_west)

    @pl.when(gy == ny_devices - 1)
    def _():
        blank(east)
        blank(eta_east)

    def exists(dx, dy):
        x, y = gx + dx, gy + dy
        return (x >= 0) & (x < nx_devices) & (y >= 0) & (y < ny_devices)

    def at_b(t):
        return {"probe": lax.rem(t, 2), "gy": lax.div(t, 2)}

    barrier = pltpu.get_barrier_semaphore()
    for dx, dy in AROUND:

        @pl.when(exists(dx, dy))
        def _():
            pl.semaphore_signal(barrier, inc=1, device_id={"gx": gx + dx, "gy": gy + dy}, device_id_type=MESH)

    def greet_a(k, carry):
        pl.semaphore_signal(barrier, inc=1, device_id={"gx": lax.rem(gx + k, group_a)}, device_id_type=MESH)
        return carry

    def greet_b(k, carry):
        pl.semaphore_signal(barrier, inc=1, device_id=at_b(lax.rem(me_b + k, group_b)), device_id_type=MESH)
        return carry

    lax.fori_loop(1, group_a, greet_a, 0)
    lax.fori_loop(1, group_b, greet_b, 0)

    for load in loads:
        load.wait()
    coupling = fric[...] * mask[...].astype(F32)
    ext[4, own_rows, :] = -coupling * vel[0]
    ext[5, own_rows, :] = -coupling * vel[1]
    ext[6, own_rows, :] = coupling
    pack_strips(ext, eta, left, right, eta_left, eta_right)

    tall = jnp.where((gx > 0) & (gx < nx_devices - 1), 3, jnp.where(nx_devices > 1, 2, 1))
    long = jnp.where((gy > 0) & (gy < ny_devices - 1), 3, jnp.where(ny_devices > 1, 2, 1))
    pl.semaphore_wait(barrier, tall * long - 1 + (group_a - 1) + (group_b - 1))

    def halo_copies(n):
        dx, dy = AROUND[n]
        to = {"gx": gx + dx, "gy": gy + dy}
        if dy == 0:
            src_row, dst_row = (ROWS, 0) if dx > 0 else (HALO, HALO + ROWS)
            main = (ext.at[:, src_row : src_row + HALO, :], ext.at[:, dst_row : dst_row + HALO, :])
            src_row, dst_row = (ROWS, 0) if dx > 0 else (ETA_HALO, ETA_HALO + ROWS)
            more = (eta.at[src_row : src_row + ETA_HALO, :], eta.at[dst_row : dst_row + ETA_HALO, :])
        else:
            strip, landing = (right, west) if dy > 0 else (left, east)
            src_row, dst_row, count = {0: (0, HALO, ROWS), 1: (ROWS - HALO, 0, HALO), -1: (0, HALO + ROWS, HALO)}[dx]
            main = (strip.at[src_row : src_row + count, :], landing.at[dst_row : dst_row + count, :])
            strip, landing = (eta_right, eta_west) if dy > 0 else (eta_left, eta_east)
            more = (strip, landing.at[1 - dx])
        return [
            pltpu.make_async_remote_copy(
                src_ref=src, dst_ref=dst, send_sem=sends.at[n], recv_sem=recvs.at[n], device_id=to, device_id_type=MESH
            )
            for (src, dst), sends, recvs in ((main, halo_send, halo_recv), (more, eta_send, eta_recv))
        ]

    for n, (dx, dy) in enumerate(AROUND):

        @pl.when(exists(dx, dy))
        def _():
            for copy in halo_copies(n):
                copy.start()

    probe_copy = pltpu.make_async_remote_copy(
        src_ref=ext.at[0:HALF, own_rows, :], dst_ref=other_probes,
        send_sem=pair_send.at[0], recv_sem=pair_recv.at[0], device_id={"probe": 1 - half}, device_id_type=MESH,
    )
    image_copy = pltpu.make_async_remote_copy(
        src_ref=natural.at[:, own_rows, :], dst_ref=other_images,
        send_sem=pair_send.at[1], recv_sem=pair_recv.at[1], device_id={"probe": 1 - half}, device_id_type=MESH,
    )

    @pl.when(half == 1)
    def _():
        probe_copy.start()

    for n, (dx, dy) in enumerate(AROUND):

        @pl.when(exists(-dx, -dy))
        def _():
            for copy in halo_copies(n):
                copy.wait_recv()

    relayout(ext, west, east, eta, eta_west, eta_east, side, eta_side, spread, eta_spread)
    coefficients(
        spread, eta_spread, coef, weight, source, state_a, gx, gy, nx_devices * ROWS, ny_devices * COLS
    )
    relax(state_a, state_b, coef, source)
    next_source(state_a, weight, source)
    relax(state_a, state_b, coef, source)
    gather_images(state_a, spread, natural)

    @pl.when(half == 0)
    def _():
        image_copy.start()

    own = products(ext, HALO, natural, HALO)

    @pl.when(half == 0)
    def _():
        probe_copy.wait_recv()
        cross = products(other_probes, 0, natural, HALO)
        message[0] = jnp.broadcast_to(own + turn(cross, 16, 1), (8, 128))

    @pl.when(half == 1)
    def _():
        message[0] = jnp.broadcast_to(turn(own, 32, 1), (8, 128))

    def reduce(phase, inbox, me, count, sends, recvs, place):
        def copy_to(k):
            return pltpu.make_async_remote_copy(
                src_ref=message.at[phase], dst_ref=inbox.at[me], send_sem=sends.at[k], recv_sem=recvs.at[me],
                device_id=place(lax.rem(me + k, count)), device_id_type=MESH,
            )

        def copy_from(k):
            return pltpu.make_async_remote_copy(
                src_ref=message.at[phase], dst_ref=inbox.at[k], send_sem=sends.at[0], recv_sem=recvs.at[k],
                device_id=place(k), device_id_type=MESH,
            )

        def send(k, carry):
            copy_to(k).start()
            return carry

        def receive(k, carry):
            copy_from(lax.rem(me + k, count)).wait_recv()
            return carry

        def sent(k, carry):
            copy_to(k).wait_send()
            return carry

        lax.fori_loop(1, count, send, 0)
        inbox[me] = message[phase]
        lax.fori_loop(1, count, receive, 0)
        total = inbox[0]
        for k in range(1, count):
            total = total + inbox[k]
        return total, lambda: lax.fori_loop(1, count, sent, 0)

    total, done_a = reduce(0, inbox_a, gx, group_a, a_send, a_recv, lambda t: {"gx": t})
    message[1] = total
    total, done_b = reduce(1, inbox_b, me_b, group_b, b_send, b_recv, at_b)
    gram[...] = total * (1.0 / (nx_devices * ROWS * ny_devices * COLS))
    images[...] = natural[:, own_rows, :]

    for n, (dx, dy) in enumerate(AROUND):

        @pl.when(exists(dx, dy))
        def _():
            for copy in halo_copies(n):
                copy.wait_send()

    done_a()
    done_b()

    @pl.when(half == 0)
    def _():
        image_copy.wait_send()

    @pl.when(half == 1)
    def _():
        probe_copy.wait_send()
        image_copy.wait_recv()


def last_kernel(sums, images, other_images, images_out, factor, gram):
    half = lax.axis_index("probe")

    def entry(i, j):
        i, j = max(i, j), min(i, j)
        if i < HALF:
            return sums[0, 4 * i + j]
        if j < HALF:
            return sums[0, 16 + 4 * (i - HALF) + j]
        return sums[0, 32 + 4 * (i - HALF) + j - HALF]

    count = 2 * HALF
    g = {(i, j): jnp.full((8, 128), entry(i, j), F32) for i in range(count) for j in range(i + 1)}
    for i in range(count):
        for j in range(i):
            if (i < HALF) == (j < HALF):
                k = 4 * (j % HALF) + i % HALF + (0 if i < HALF else 32)
                g[i, j] = 0.5 * (g[i, j] + jnp.full((8, 128), sums[0, k], F32))
    lane, sub = lanes(), sublanes()
    out = jnp.zeros((8, 128), F32)
    for i in range(count):
        row = jnp.zeros((8, 128), F32)
        for j in range(count):
            a, b = i % HALF, j % HALF
            if (i < HALF) == (j < HALF):
                value = sums[0, 4 * a + b + (0 if i < HALF else 32)]
            else:
                value = entry(i, j)
            row = jnp.where(lane == j, value, row)
        out = jnp.where(sub == i, row, out)
    gram[...] = out[:, :count]

    low, inverse = {}, {}
    for j in range(count):
        for i in range(j, count):
            value = g[i, j]
            for k in range(j):
                value = value - low[i, k] * low[j, k]
            if i == j:
                root = jnp.sqrt(value)
                inverse[j] = 1.0 / root
            else:
                low[i, j] = value * inverse[j]

    def solve(sources, out_rows):
        def part(k):
            rows = pl.ds(8 * k, 8)
            done = []
            for i, (ref, p) in enumerate(sources):
                value = ref[p, rows, :]
                for j in range(i):
                    value = value - low[i, j] * done[j]
                value = value * inverse[i]
                done.append(value)
                if i >= len(sources) - HALF:
                    factor[i - len(sources) + HALF, rows, :] = value

        unrolled(ROWS // 8, part)

    images_out[...] = images[...]

    @pl.when(half == 0)
    def _():
        solve([(images, p) for p in range(HALF)], 0)

    @pl.when(half == 1)
    def _():
        solve([(other_images, p) for p in range(HALF)] + [(images, p) for p in range(HALF)], HALF)


def body(probes, velocity, eta, friction, noise, ice):
    nx_devices, ny_devices = lax.axis_size("gx"), lax.axis_size("gy")
    vmem = lambda *shape: pltpu.VMEM(shape, F32)
    dma = lambda count: pltpu.SemaphoreType.DMA((count,))
    grid = (BI, BJ, 8, 128)
    padded = (BI + 2, BJ + 2, 8, 128)
    whole = pl.BlockSpec(memory_space=pltpu.VMEM)
    tile = jax.ShapeDtypeStruct((HALF, ROWS, COLS), F32)
    group_a, group_b = nx_devices, 2 * ny_devices
    images, other_images, sums = pl.pallas_call(
        functools.partial(main_kernel, nx_devices, ny_devices),
        out_shape=(tile, tile, jax.ShapeDtypeStruct((8, 128), F32)),
        in_specs=[pl.BlockSpec(memory_space=pl.ANY)] * 6,
        out_specs=(whole, whole, whole),
        scratch_shapes=[
            vmem(8, EXT, 128), vmem(EXT, 128), vmem(EXT, 128), vmem(ROWS, 128), vmem(ROWS, 128),
            vmem(ROWS + 2 * ETA_HALO, 128), vmem(3, 16, 128), vmem(3, 16, 128), vmem(16, 128), vmem(16, 128),
            vmem(2, ROWS, COLS), vmem(ROWS, COLS), pltpu.VMEM((ROWS, COLS), jnp.int32),
            vmem(2, EXT, 128), vmem(ROWS + 2 * ETA_HALO, 128),
            vmem(5, *grid), vmem(*padded), vmem(16, *grid), vmem(2, *grid), vmem(2, *grid),
            vmem(2, *padded), vmem(2, *padded),
            vmem(HALF, EXT, 128), vmem(HALF, ROWS, COLS), vmem(2, 8, 128), vmem(group_a, 8, 128), vmem(group_b, 8, 128),
            dma(6), dma(8), dma(8), dma(8), dma(8), dma(2), dma(2),
            dma(group_a), dma(group_a), dma(group_b), dma(group_b),
        ],
        compiler_params=pltpu.CompilerParams(
            collective_id=0, has_side_effects=True, vmem_limit_bytes=32 * 1024 * 1024
        ),
    )(probes, velocity, eta, friction, noise, ice)
    return pl.pallas_call(
        last_kernel,
        out_shape=(tile, tile, jax.ShapeDtypeStruct((2 * HALF, 2 * HALF), F32)),
        in_specs=[pl.BlockSpec(memory_space=pltpu.SMEM), whole, whole],
        out_specs=(whole, whole, whole),
    )(sums, images, other_images)


def solution(mesh):
    in_specs = (
        P("probe", "gx", "gy"),
        P(None, "gx", "gy"),
        P("gx", "gy"),
        P("gx", "gy"),
        P("gx", "gy"),
        P("gx", "gy"),
    )
    out_specs = (P("probe", "gx", "gy"), P("probe", "gx", "gy"), P())
    return jax.shard_map(body, mesh=mesh, in_specs=in_specs, out_specs=out_specs, check_vma=False)
```

```python
import functools

import jax
import jax.numpy as jnp
import numpy as np
from jax import lax
from jax.experimental import pallas as pl
from jax.experimental.pallas import tpu as pltpu
from jax.sharding import PartitionSpec as P

SWEEPS = 9
OMEGA = 0.6
DRAG = 0.05
PRIOR = 0.05

HALF = 4
ROWS, COLS = 64, 128
HALO = 2 * (SWEEPS - 1)
BI, BJ = (ROWS + 2 * HALO) // 8, (COLS + 2 * HALO) // 32
EXT = ROWS + 2 * HALO
ETA_HALO = 24
MESH = pl.DeviceIdType.MESH
F32 = jnp.float32
SERIES = np.polynomial.Polynomial([0.0])
for power in range(SWEEPS):
    SERIES = SERIES + np.polynomial.Polynomial([1.0 - OMEGA, OMEGA]) ** power
SERIES = [float(a) for a in SERIES.coef]
AROUND = ((-1, 0), (1, 0), (0, -1), (0, 1), (-1, -1), (-1, 1), (1, -1), (1, 1))


def lanes():
    return lax.broadcasted_iota(jnp.int32, (8, 128), 1)


def sublanes():
    return lax.broadcasted_iota(jnp.int32, (8, 128), 0)


def turn(x, shift, axis):
    shift = shift % x.shape[axis]
    return pltpu.roll(x, shift, axis) if shift else x


def pick(x, index):
    return jnp.take_along_axis(x, index, axis=1, mode="promise_in_bounds")


def unrolled(count, body, start=0):
    def step(i, carry):
        body(i)
        return carry

    lax.fori_loop(start, count, step, 0, unroll=True)


def ends_first(body):
    body(0)
    body(BI - 1)
    unrolled(BI - 1, body, 1)


def pack_strips(ext, eta, left, right, eta_left, eta_right):
    lane = lax.broadcasted_iota(jnp.int32, (ROWS, COLS), 1)
    for f in range(8):
        own = ext[f, HALO : HALO + ROWS, :]
        here = (lane >= 16 * f) & (lane < 16 * f + 16)
        first, last = turn(own, 16 * f, 1), turn(own, 16 * f + 16, 1)
        left[...] = first if f == 0 else jnp.where(here, first, left[...])
        right[...] = last if f == 0 else jnp.where(here, last, right[...])
    lane = lax.broadcasted_iota(jnp.int32, (16, COLS), 1)
    first = last = None
    for g in range(4):
        own = eta[ETA_HALO + 16 * g : ETA_HALO + 16 * g + 16, :]
        here = (lane >= 32 * g) & (lane < 32 * g + 32)
        a, b = turn(own, 32 * g, 1), turn(own, 32 * g + 32, 1)
        first = a if g == 0 else jnp.where(here, a, first)
        last = b if g == 0 else jnp.where(here, b, last)
    eta_left[...] = first
    eta_right[...] = last


def places(j):
    col = BJ * (lanes() & 31) + j - HALO
    return col, jnp.clip(col, 0, COLS - 1), (col < 0) | (col >= COLS)


def relayout_own(ext, eta, spread, eta_spread):
    group = lanes() >> 5

    def fields(i):
        rows = pl.ds(i, 8, stride=BI)
        own = [ext[f, rows, :] for f in range(8)]
        for j in range(BJ):
            _, at, _ = places(j)
            value = pick(own[HALF - 1], at)
            for p in range(HALF - 2, -1, -1):
                value = jnp.where(group == p, pick(own[p], at), value)
            spread[0, i, j] = value
            for f in range(4):
                spread[1 + f, i, j] = pick(own[4 + f], at)

    unrolled(BI, fields)

    def viscosity(i):
        own = eta[pl.ds(i + ETA_HALO - HALO - 1, 8, stride=BI), :]
        for j in range(-1, BJ + 1):
            eta_spread[i, j + 1] = pick(own, places(j)[1])

    unrolled(BI + 2, viscosity)


def relayout_sides(west, east, eta_west, eta_east, side, eta_side, spread, eta_spread):
    lane = lanes()
    group = lane >> 5
    wide = lax.broadcasted_iota(jnp.int32, (EXT, COLS), 1)
    w, e = west[...], east[...]
    side[0] = jnp.where(wide < 64, w, turn(e, 64, 1))
    side[1] = jnp.where(wide < 64, turn(w, 64, 1), e)
    for k in range(14):
        own_row = 8 * k - ETA_HALO
        slot = 0 if own_row < 0 else (1 if own_row < ROWS else 2)
        row = own_row - ROWS * (slot - 1)
        g, r = row // 16, row % 16
        a = turn(eta_west[slot, r : r + 8, :], -32 * g, 1)
        b = turn(eta_east[slot, r : r + 8, :], 32 - 32 * g, 1)
        eta_side[8 * k : 8 * k + 8, :] = jnp.where(lane < 32, a, b)

    def viscosity(i):
        beside = eta_side[pl.ds(i + ETA_HALO - HALO - 1, 8, stride=BI), :]
        for j in range(-1, BJ + 1):
            col, _, outside = places(j)
            at = jnp.where(outside, jnp.where(col < 0, col + 32, col - COLS + 32), 0)
            eta_spread[i, j + 1] = jnp.where(outside, pick(beside, at), eta_spread[i, j + 1])

    unrolled(BI + 2, viscosity)

    def fields(i):
        rows = pl.ds(i, 8, stride=BI)
        low, high = side[0, rows, :], side[1, rows, :]
        for j in range(BJ):
            col, _, outside = places(j)
            at = jnp.where(outside, jnp.where(col < 0, col + HALO, col - COLS + 64), 0)
            spread[0, i, j] = jnp.where(outside, pick(low, at + 16 * group), spread[0, i, j])
            for f in range(4):
                spread[1 + f, i, j] = jnp.where(outside, pick(high, at + 16 * f), spread[1 + f, i, j])

    unrolled(BI, fields)


def store_state(state, c, i, values):
    values = [turn(values[BJ - 1], 1, 1)] + values + [turn(values[0], -1, 1)]
    for j, value in enumerate(values):
        state[c, i + 1, j] = value
    if isinstance(i, int):
        for j, value in enumerate(values):
            if i == 0:
                state[c, BI + 1, j] = turn(value, -1, 0)
            else:
                state[c, 0, j] = turn(value, 1, 0)


def coefficients(spread, eta_spread, coef, weight, source, state, gx, gy, nx, ny):
    lane, sub = lanes(), sublanes()

    def row(i):
        r = gx * ROWS - HALO + BI * sub + i
        row_in = (r >= 0) & (r < nx)
        first, second = [], []
        for j in range(BJ):
            c = gy * COLS - HALO + BJ * (lane & 31) + j
            inside = row_in & (c >= 0) & (c < ny)
            m = eta_spread[i + 1, j + 1]
            e, w = eta_spread[i + 2, j + 1], eta_spread[i, j + 1]
            n, s = eta_spread[i + 1, j + 2], eta_spread[i + 1, j]
            react = spread[3, i, j] + DRAG
            me, mw, mn, ms = m + e, m + w, m + n, m + s
            along, across = me + mw, mn + ms
            w1 = jnp.where(inside, 1.0 / (2.0 * along + 0.5 * across + react), 0.0)
            w2 = jnp.where(inside, 1.0 / (0.5 * along + 2.0 * across + react), 0.0)
            a1, b1, q1 = 2.0 * w1, 0.5 * w1, 0.25 * w1
            a2, b2, q2 = 2.0 * w2, 0.5 * w2, 0.25 * w2
            coef[0, i, j] = a1 * me
            coef[1, i, j] = a1 * mw
            coef[2, i, j] = b1 * mn
            coef[3, i, j] = b1 * ms
            be, bw, qn, qs = b1 * e, b1 * w, q1 * n, q1 * s
            coef[4, i, j] = be + qn
            coef[5, i, j] = be + qs
            coef[6, i, j] = bw + qn
            coef[7, i, j] = bw + qs
            coef[8, i, j] = b2 * me
            coef[9, i, j] = b2 * mw
            coef[10, i, j] = a2 * mn
            coef[11, i, j] = a2 * ms
            bn, bs, qe, qw = b2 * n, b2 * s, q2 * e, q2 * w
            coef[12, i, j] = bn + qe
            coef[13, i, j] = bs + qe
            coef[14, i, j] = bn + qw
            coef[15, i, j] = bs + qw
            w1, w2 = OMEGA * w1, OMEGA * w2
            noise = spread[4, i, j]
            weight[0, i, j] = w1 * noise
            weight[1, i, j] = w2 * noise
            probe = spread[0, i, j]
            f1, f2 = w1 * (spread[1, i, j] * probe), w2 * (spread[2, i, j] * probe)
            source[0, i, j] = f1
            source[1, i, j] = f2
            first.append(SERIES[-1] * f1)
            second.append(SERIES[-1] * f2)
        store_state(state, 0, i, first)
        store_state(state, 1, i, second)

    ends_first(row)


def sweep(old, new, coef, source, factor):
    def row(i):
        first, second = [], []
        for j in range(BJ):

            def at(c, di, dj):
                return old[c, i + 1 + di, j + 1 + dj]

            k = [coef[n, i, j] for n in range(16)]
            first.append(
                factor * source[0, i, j]
                + (k[0] * at(0, 1, 0) + k[1] * at(0, -1, 0))
                + (k[2] * at(0, 0, 1) + k[3] * at(0, 0, -1))
                + (k[4] * at(1, 1, 1) - k[5] * at(1, 1, -1))
                + (k[7] * at(1, -1, -1) - k[6] * at(1, -1, 1))
            )
            second.append(
                factor * source[1, i, j]
                + (k[8] * at(1, 1, 0) + k[9] * at(1, -1, 0))
                + (k[10] * at(1, 0, 1) + k[11] * at(1, 0, -1))
                + (k[12] * at(0, 1, 1) - k[13] * at(0, 1, -1))
                + (k[15] * at(0, -1, -1) - k[14] * at(0, -1, 1))
            )
        store_state(new, 0, i, first)
        store_state(new, 1, i, second)

    ends_first(row)


def relax_twice(state_a, state_b, coef, weight, source):
    def step(k, carry):
        second = (k & 1) == 1
        for n in range((SWEEPS - 1) // 2):
            factor = jnp.where(second, SERIES[(SWEEPS - 1) // 2 - 1 - n], SERIES[SWEEPS - 2 - n])
            old, new = (state_a, state_b) if n % 2 == 0 else (state_b, state_a)
            sweep(old, new, coef, source, factor)

        @pl.when(k == 1)
        def _():
            next_source(state_a, weight, source)

        return carry

    lax.fori_loop(0, 4, step, 0)


def next_source(state, weight, source):
    def row(i):
        for c in range(2):
            values = [weight[c, i, j] * state[c, i + 1, j + 1] for j in range(BJ)]
            for j in range(BJ):
                source[c, i, j] = values[j]
            store_state(state, c, i, [SERIES[-1] * value for value in values])

    ends_first(row)


def gather_images(state, spread, natural):
    lane = lanes()
    place = lane + HALO
    block = (place * 205) >> 10
    rest = place - BJ * block

    def row(i):
        values = [
            spread[1, i, j] * state[0, i + 1, j + 1]
            + spread[2, i, j] * state[1, i + 1, j + 1]
            + PRIOR * spread[0, i, j]
            for j in range(BJ)
        ]
        for p in range(HALF):
            out = pick(values[0], block + 32 * p)
            for j in range(1, BJ):
                out = jnp.where(rest == j, pick(values[j], block + 32 * p), out)
            natural[p, pl.ds(i, 8, stride=BI), :] = out

    unrolled(BI, row)


def products(left, left_row, right, right_row):
    def add(k, totals):
        a = [left[p, pl.ds(left_row + 8 * k, 8), :] for p in range(HALF)]
        b = [right[p, pl.ds(right_row + 8 * k, 8), :] for p in range(HALF)]
        return tuple(t + a[n // 4] * b[n % 4] for n, t in enumerate(totals))

    zero = jnp.zeros((8, 128), F32)
    totals = lax.fori_loop(0, ROWS // 8, add, (zero,) * 16, unroll=True)
    sums = jnp.concatenate([jnp.sum(t, axis=0, keepdims=True) for t in totals], axis=0)
    sums = jnp.sum(sums, axis=1, keepdims=True)
    lane = lax.broadcasted_iota(jnp.int32, (16, 128), 1)
    row = lax.broadcasted_iota(jnp.int32, (16, 128), 0)
    return jnp.sum(jnp.where(lane == row, sums, 0.0), axis=0, keepdims=True)


def main_kernel(
    nx_devices, ny_devices,
    probes, velocity, eta_in, friction, noise, ice,
    images, other_images, gram,
    ext, west, east, left, right, eta, eta_west, eta_east, eta_left, eta_right,
    vel, fric, mask, side, eta_side, spread, eta_spread, coef, weight, source, state_a, state_b,
    natural, other_probes, message, inbox_a, inbox_b,
    in_sem, halo_send, halo_recv, eta_send, eta_recv, pair_send, pair_recv,
    a_send, a_recv, b_send, b_recv, near_a, near_b,
):
    half, gx, gy = lax.axis_index("probe"), lax.axis_index("gx"), lax.axis_index("gy")
    group_a, group_b = nx_devices, 2 * ny_devices
    me_b = gy * 2 + half
    own_rows = slice(HALO, HALO + ROWS)

    loads = [
        pltpu.make_async_copy(velocity, vel, in_sem.at[0]),
        pltpu.make_async_copy(friction, fric, in_sem.at[1]),
        pltpu.make_async_copy(ice, mask, in_sem.at[2]),
        pltpu.make_async_copy(probes, ext.at[0:HALF, own_rows, :], in_sem.at[3]),
        pltpu.make_async_copy(noise, ext.at[7, own_rows, :], in_sem.at[4]),
        pltpu.make_async_copy(eta_in, eta.at[ETA_HALO : ETA_HALO + ROWS, :], in_sem.at[5]),
    ]
    for load in loads:
        load.start()

    def blank(ref):
        ref[...] = jnp.zeros(ref.shape, F32)

    @pl.when(gx == 0)
    def _():
        blank(ext.at[:, 0:HALO, :])
        blank(eta.at[0:ETA_HALO, :])
        for ref in (west, east):
            blank(ref.at[0:HALO, :])
        for ref in (eta_west, eta_east):
            blank(ref.at[0])

    @pl.when(gx == nx_devices - 1)
    def _():
        blank(ext.at[:, HALO + ROWS : EXT, :])
        blank(eta.at[ETA_HALO + ROWS : 2 * ETA_HALO + ROWS, :])
        for ref in (west, east):
            blank(ref.at[HALO + ROWS : EXT, :])
        for ref in (eta_west, eta_east):
            blank(ref.at[2])

    @pl.when(gy == 0)
    def _():
        blank(west)
        blank(eta_west)

    @pl.when(gy == ny_devices - 1)
    def _():
        blank(east)
        blank(eta_east)

    def exists(dx, dy):
        x, y = gx + dx, gy + dy
        return (x >= 0) & (x < nx_devices) & (y >= 0) & (y < ny_devices)

    def at_b(t):
        return {"probe": lax.rem(t, 2), "gy": lax.div(t, 2)}

    def along_x(step):
        return {"gx": lax.rem(gx + step + nx_devices, nx_devices)}

    def along_y(step):
        return {"gy": lax.rem(gy + step + ny_devices, ny_devices)}

    partner = {"probe": 1 - half}

    def signal(semaphore, to):
        pl.semaphore_signal(semaphore, inc=1, device_id=to, device_id_type=MESH)

    barrier = pltpu.get_barrier_semaphore()
    for dx, dy in AROUND:

        @pl.when(exists(dx, dy))
        def _():
            signal(barrier, {"gx": gx + dx, "gy": gy + dy})

    first_x, last_x = gx == 0, gx == nx_devices - 1
    first_y, last_y = gy == 0, gy == ny_devices - 1

    @pl.when(first_x | last_x)
    def _():
        signal(barrier, {"gx": nx_devices - 1 - gx})

    @pl.when(first_y | last_y)
    def _():
        signal(barrier, {"gy": ny_devices - 1 - gy})

    signal(barrier, partner)

    def relay(stage):
        for step in (-(2**stage), 2**stage):
            signal(near_a.at[stage], along_x(step))
            if stage < 2:
                signal(near_b.at[stage], along_y(step))
        signal(near_b.at[stage], partner)

    def hear(stage):
        pl.semaphore_wait(near_a.at[stage], 2)
        pl.semaphore_wait(near_b.at[stage], 3 if stage < 2 else 1)

    for load in loads:
        load.wait()
    coupling = fric[...] * mask[...].astype(F32)
    ext[4, own_rows, :] = -coupling * vel[0]
    ext[5, own_rows, :] = -coupling * vel[1]
    ext[6, own_rows, :] = coupling
    pack_strips(ext, eta, left, right, eta_left, eta_right)

    edge_x, edge_y = (first_x | last_x).astype(jnp.int32), (first_y | last_y).astype(jnp.int32)
    pl.semaphore_wait(barrier, (3 - edge_x) * (3 - edge_y) + edge_x + edge_y)

    def halo_copies(n):
        dx, dy = AROUND[n]
        to = {"gx": gx + dx, "gy": gy + dy}
        if dy == 0:
            src_row, dst_row = (ROWS, 0) if dx > 0 else (HALO, HALO + ROWS)
            main = (ext.at[:, src_row : src_row + HALO, :], ext.at[:, dst_row : dst_row + HALO, :])
            src_row, dst_row = (ROWS, 0) if dx > 0 else (ETA_HALO, ETA_HALO + ROWS)
            more = (eta.at[src_row : src_row + ETA_HALO, :], eta.at[dst_row : dst_row + ETA_HALO, :])
        else:
            strip, landing = (right, west) if dy > 0 else (left, east)
            src_row, dst_row, count = {0: (0, HALO, ROWS), 1: (ROWS - HALO, 0, HALO), -1: (0, HALO + ROWS, HALO)}[dx]
            main = (strip.at[src_row : src_row + count, :], landing.at[dst_row : dst_row + count, :])
            strip, landing = (eta_right, eta_west) if dy > 0 else (eta_left, eta_east)
            more = (strip, landing.at[1 - dx])
        return [
            pltpu.make_async_remote_copy(
                src_ref=src, dst_ref=dst, send_sem=sends.at[n], recv_sem=recvs.at[n], device_id=to, device_id_type=MESH
            )
            for (src, dst), sends, recvs in ((main, halo_send, halo_recv), (more, eta_send, eta_recv))
        ]

    for n, (dx, dy) in enumerate(AROUND):

        @pl.when(exists(dx, dy))
        def _():
            for copy in halo_copies(n):
                copy.start()

    relay(0)

    probe_copy = pltpu.make_async_remote_copy(
        src_ref=ext.at[0:HALF, own_rows, :], dst_ref=other_probes,
        send_sem=pair_send.at[0], recv_sem=pair_recv.at[0], device_id={"probe": 1 - half}, device_id_type=MESH,
    )
    image_copy = pltpu.make_async_remote_copy(
        src_ref=natural.at[:, own_rows, :], dst_ref=other_images,
        send_sem=pair_send.at[1], recv_sem=pair_recv.at[1], device_id={"probe": 1 - half}, device_id_type=MESH,
    )

    def await_halos(directions):
        for n in directions:
            dx, dy = AROUND[n]

            @pl.when(exists(-dx, -dy))
            def _():
                for copy in halo_copies(n):
                    copy.wait_recv()

    await_halos((0, 1))
    relayout_own(ext, eta, spread, eta_spread)
    await_halos(range(2, 8))

    @pl.when(half == 1)
    def _():
        probe_copy.start()

    hear(0)
    relay(1)
    relayout_sides(west, east, eta_west, eta_east, side, eta_side, spread, eta_spread)
    coefficients(
        spread, eta_spread, coef, weight, source, state_a, gx, gy, nx_devices * ROWS, ny_devices * COLS
    )
    hear(1)
    relay(2)
    relax_twice(state_a, state_b, coef, weight, source)
    gather_images(state_a, spread, natural)

    @pl.when(half == 0)
    def _():
        image_copy.start()

    hear(2)
    own = products(ext, HALO, natural, HALO)

    @pl.when(half == 0)
    def _():
        probe_copy.wait_recv()
        cross = products(other_probes, 0, natural, HALO)
        message[0] = own + turn(cross, 16, 1)

    @pl.when(half == 1)
    def _():
        message[0] = turn(own, 32, 1)

    def reduce(phase, inbox, me, count, sends, recvs, place):
        def copy_to(k):
            return pltpu.make_async_remote_copy(
                src_ref=message.at[phase], dst_ref=inbox.at[me], send_sem=sends.at[k], recv_sem=recvs.at[me],
                device_id=place(lax.rem(me + k, count)), device_id_type=MESH,
            )

        def copy_from(k):
            return pltpu.make_async_remote_copy(
                src_ref=message.at[phase], dst_ref=inbox.at[k], send_sem=sends.at[0], recv_sem=recvs.at[k],
                device_id=place(k), device_id_type=MESH,
            )

        def send(k, carry):
            copy_to(k).start()
            return carry

        def receive(k, carry):
            copy_from(lax.rem(me + k, count)).wait_recv()
            return carry

        def sent(k, carry):
            copy_to(k).wait_send()
            return carry

        lax.fori_loop(1, count, send, 0)
        inbox[me] = message[phase]
        if phase == 0:
            images[...] = natural[:, own_rows, :]
        lax.fori_loop(1, count, receive, 0)
        total = inbox[0]
        for k in range(1, count):
            total = total + inbox[k]
        return total, lambda: lax.fori_loop(1, count, sent, 0)

    total, done_a = reduce(0, inbox_a, gx, group_a, a_send, a_recv, lambda t: {"gx": t})
    message[1] = total
    total, done_b = reduce(1, inbox_b, me_b, group_b, b_send, b_recv, at_b)
    gram[...] = jnp.broadcast_to(total * (1.0 / (nx_devices * ROWS * ny_devices * COLS)), (8, 128))

    for n, (dx, dy) in enumerate(AROUND):

        @pl.when(exists(dx, dy))
        def _():
            for copy in halo_copies(n):
                copy.wait_send()

    done_a()
    done_b()

    @pl.when(half == 0)
    def _():
        image_copy.wait_send()

    @pl.when(half == 1)
    def _():
        probe_copy.wait_send()
        image_copy.wait_recv()


def last_kernel(sums, images, other_images, images_out, factor, gram, factor_here, gram_here, sems):
    half = lax.axis_index("probe")
    images_copy = pltpu.make_async_copy(images, images_out, sems.at[0])
    images_copy.start()

    lane, sub = lanes(), sublanes()
    low_row, low_col = sub < HALF, lane < HALF
    a, b = sub & (HALF - 1), lane & (HALF - 1)
    at = jnp.where(low_row == low_col, HALF * a + b, jnp.where(low_col, HALF * a + b, HALF * b + a))
    at = at + jnp.where(low_row == low_col, jnp.where(low_row, 0, 2 * HALF * HALF), HALF * HALF)
    row = sums[...]
    full = pick(row, jnp.where(lane < 2 * HALF, at, 0))
    gram_here[...] = full[:, : 2 * HALF]
    gram_copy = pltpu.make_async_copy(gram_here, gram, sems.at[1])
    gram_copy.start()

    def entry(i, j):
        k = HALF * (i % HALF) + j % HALF
        if (i < HALF) == (j < HALF):
            return jnp.broadcast_to(row[:, (k if i < HALF else k + 32) :][:, :1], (8, 128))
        return jnp.broadcast_to(row[:, k + 16 :][:, :1], (8, 128))

    count = 2 * HALF
    low, inverse = {}, {}
    for j in range(count):
        for i in range(j, count):
            value = entry(i, j)
            if i != j and (i < HALF) == (j < HALF):
                value = 0.5 * (value + entry(j, i))
            for k in range(j):
                value = value - low[i, k] * low[j, k]
            if i == j:
                guess = lax.rsqrt(value)
                inverse[j] = guess * (1.5 - 0.5 * value * guess * guess)
            else:
                low[i, j] = value * inverse[j]

    def solve(sources):
        def part(k):
            rows = pl.ds(8 * k, 8)
            done = []
            for i, (ref, p) in enumerate(sources):
                value = ref[p, rows, :]
                for j in range(i):
                    value = value - low[i, j] * done[j]
                value = value * inverse[i]
                done.append(value)
                if i >= len(sources) - HALF:
                    factor_here[i - len(sources) + HALF, rows, :] = value

        unrolled(ROWS // 8, part)

    @pl.when(half == 0)
    def _():
        solve([(images, p) for p in range(HALF)])

    @pl.when(half == 1)
    def _():
        solve([(other_images, p) for p in range(HALF)] + [(images, p) for p in range(HALF)])

    factor_copy = pltpu.make_async_copy(factor_here, factor, sems.at[2])
    factor_copy.start()
    images_copy.wait()
    gram_copy.wait()
    factor_copy.wait()


def body(probes, velocity, eta, friction, noise, ice):
    nx_devices, ny_devices = lax.axis_size("gx"), lax.axis_size("gy")
    vmem = lambda *shape: pltpu.VMEM(shape, F32)
    dma = lambda count: pltpu.SemaphoreType.DMA((count,))
    grid = (BI, BJ, 8, 128)
    padded = (BI + 2, BJ + 2, 8, 128)
    whole = pl.BlockSpec(memory_space=pltpu.VMEM)
    tile = jax.ShapeDtypeStruct((HALF, ROWS, COLS), F32)
    group_a, group_b = nx_devices, 2 * ny_devices
    images, other_images, sums = pl.pallas_call(
        functools.partial(main_kernel, nx_devices, ny_devices),
        out_shape=(tile, tile, jax.ShapeDtypeStruct((8, 128), F32)),
        in_specs=[pl.BlockSpec(memory_space=pl.ANY)] * 6,
        out_specs=(whole, whole, whole),
        scratch_shapes=[
            vmem(8, EXT, 128), vmem(EXT, 128), vmem(EXT, 128), vmem(ROWS, 128), vmem(ROWS, 128),
            vmem(ROWS + 2 * ETA_HALO, 128), vmem(3, 16, 128), vmem(3, 16, 128), vmem(16, 128), vmem(16, 128),
            vmem(2, ROWS, COLS), vmem(ROWS, COLS), pltpu.VMEM((ROWS, COLS), jnp.int32),
            vmem(2, EXT, 128), vmem(ROWS + 2 * ETA_HALO, 128),
            vmem(5, *grid), vmem(*padded), vmem(16, *grid), vmem(2, *grid), vmem(2, *grid),
            vmem(2, *padded), vmem(2, *padded),
            vmem(HALF, EXT, 128), vmem(HALF, ROWS, COLS), vmem(2, 1, 128), vmem(group_a, 1, 128), vmem(group_b, 1, 128),
            dma(6), dma(8), dma(8), dma(8), dma(8), dma(2), dma(2),
            dma(group_a), dma(group_a), dma(group_b), dma(group_b),
            pltpu.SemaphoreType.REGULAR((3,)), pltpu.SemaphoreType.REGULAR((3,)),
        ],
        compiler_params=pltpu.CompilerParams(
            collective_id=0, has_side_effects=True, vmem_limit_bytes=32 * 1024 * 1024
        ),
    )(*[pltpu.with_memory_space_constraint(x, pltpu.HBM) for x in (probes, velocity, eta, friction, noise, ice)])
    square = (2 * HALF, 2 * HALF)
    return pl.pallas_call(
        last_kernel,
        out_shape=(tile, tile, jax.ShapeDtypeStruct(square, F32)),
        in_specs=[whole, whole, whole],
        out_specs=(pl.BlockSpec(memory_space=pl.ANY),) * 3,
        scratch_shapes=[vmem(HALF, ROWS, COLS), vmem(*square), dma(3)],
        compiler_params=pltpu.CompilerParams(vmem_limit_bytes=16 * 1024 * 1024),
    )(sums, images, other_images)


def solution(mesh):
    in_specs = (
        P("probe", "gx", "gy"),
        P(None, "gx", "gy"),
        P("gx", "gy"),
        P("gx", "gy"),
        P("gx", "gy"),
        P("gx", "gy"),
    )
    out_specs = (P("probe", "gx", "gy"), P("probe", "gx", "gy"), P())
    return jax.shard_map(body, mesh=mesh, in_specs=in_specs, out_specs=out_specs, check_vma=False)
```

```python
import functools

import jax
import jax.numpy as jnp
import numpy as np
from jax import lax
from jax.experimental import pallas as pl
from jax.experimental.pallas import tpu as pltpu
from jax.sharding import PartitionSpec as P

SWEEPS = 9
OMEGA = 0.6
DRAG = 0.05
PRIOR = 0.05

HALF = 4
ROWS, COLS = 64, 128
HALO = 2 * (SWEEPS - 1)
BI, BJ = (ROWS + 2 * HALO) // 8, (COLS + 2 * HALO) // 32
EXT = ROWS + 2 * HALO
ETA_HALO = 24
MESH = pl.DeviceIdType.MESH
F32 = jnp.float32
SERIES = np.polynomial.Polynomial([0.0])
for power in range(SWEEPS):
    SERIES = SERIES + np.polynomial.Polynomial([1.0 - OMEGA, OMEGA]) ** power
SERIES = [float(a) for a in SERIES.coef]
AROUND = ((-1, 0), (1, 0), (0, -1), (0, 1), (-1, -1), (-1, 1), (1, -1), (1, 1))


def lanes():
    return lax.broadcasted_iota(jnp.int32, (8, 128), 1)


def sublanes():
    return lax.broadcasted_iota(jnp.int32, (8, 128), 0)


def turn(x, shift, axis):
    shift = shift % x.shape[axis]
    return pltpu.roll(x, shift, axis) if shift else x


def pick(x, index):
    return jnp.take_along_axis(x, index, axis=1, mode="promise_in_bounds")


def unrolled(count, body, start=0):
    def step(i, carry):
        body(i)
        return carry

    lax.fori_loop(start, count, step, 0, unroll=True)


def ends_first(body):
    body(0)
    body(BI - 1)
    unrolled(BI - 1, body, 1)


def pack_strips(ext, eta, left, right, eta_left, eta_right):
    lane = lax.broadcasted_iota(jnp.int32, (ROWS, COLS), 1)
    for f in range(8):
        own = ext[f, HALO : HALO + ROWS, :]
        here = (lane >= 16 * f) & (lane < 16 * f + 16)
        first, last = turn(own, 16 * f, 1), turn(own, 16 * f + 16, 1)
        left[...] = first if f == 0 else jnp.where(here, first, left[...])
        right[...] = last if f == 0 else jnp.where(here, last, right[...])
    lane = lax.broadcasted_iota(jnp.int32, (16, COLS), 1)
    first = last = None
    for g in range(4):
        own = eta[ETA_HALO + 16 * g : ETA_HALO + 16 * g + 16, :]
        here = (lane >= 32 * g) & (lane < 32 * g + 32)
        a, b = turn(own, 32 * g, 1), turn(own, 32 * g + 32, 1)
        first = a if g == 0 else jnp.where(here, a, first)
        last = b if g == 0 else jnp.where(here, b, last)
    eta_left[...] = first
    eta_right[...] = last


def places(j):
    col = BJ * (lanes() & 31) + j - HALO
    return col, jnp.clip(col, 0, COLS - 1), (col < 0) | (col >= COLS)


def relayout_own(ext, eta, spread, eta_spread):
    group = lanes() >> 5

    def fields(i):
        rows = pl.ds(i, 8, stride=BI)
        own = [ext[f, rows, :] for f in range(8)]
        for j in range(BJ):
            _, at, _ = places(j)
            value = pick(own[HALF - 1], at)
            for p in range(HALF - 2, -1, -1):
                value = jnp.where(group == p, pick(own[p], at), value)
            spread[0, i, j] = value
            for f in range(4):
                spread[1 + f, i, j] = pick(own[4 + f], at)

    unrolled(BI, fields)

    def viscosity(i):
        own = eta[pl.ds(i + ETA_HALO - HALO - 1, 8, stride=BI), :]
        for j in range(-1, BJ + 1):
            eta_spread[i, j + 1] = pick(own, places(j)[1])

    unrolled(BI + 2, viscosity)


def relayout_sides(west, east, eta_west, eta_east, side, eta_side, spread, eta_spread):
    lane = lanes()
    group = lane >> 5
    wide = lax.broadcasted_iota(jnp.int32, (EXT, COLS), 1)
    w, e = west[...], east[...]
    side[0] = jnp.where(wide < 64, w, turn(e, 64, 1))
    side[1] = jnp.where(wide < 64, turn(w, 64, 1), e)
    for k in range(14):
        own_row = 8 * k - ETA_HALO
        slot = 0 if own_row < 0 else (1 if own_row < ROWS else 2)
        row = own_row - ROWS * (slot - 1)
        g, r = row // 16, row % 16
        a = turn(eta_west[slot, r : r + 8, :], -32 * g, 1)
        b = turn(eta_east[slot, r : r + 8, :], 32 - 32 * g, 1)
        eta_side[8 * k : 8 * k + 8, :] = jnp.where(lane < 32, a, b)

    def viscosity(i):
        beside = eta_side[pl.ds(i + ETA_HALO - HALO - 1, 8, stride=BI), :]
        for j in range(-1, BJ + 1):
            col, _, outside = places(j)
            at = jnp.where(outside, jnp.where(col < 0, col + 32, col - COLS + 32), 0)
            eta_spread[i, j + 1] = jnp.where(outside, pick(beside, at), eta_spread[i, j + 1])

    unrolled(BI + 2, viscosity)

    def fields(i):
        rows = pl.ds(i, 8, stride=BI)
        low, high = side[0, rows, :], side[1, rows, :]
        for j in range(BJ):
            col, _, outside = places(j)
            at = jnp.where(outside, jnp.where(col < 0, col + HALO, col - COLS + 64), 0)
            spread[0, i, j] = jnp.where(outside, pick(low, at + 16 * group), spread[0, i, j])
            for f in range(4):
                spread[1 + f, i, j] = jnp.where(outside, pick(high, at + 16 * f), spread[1 + f, i, j])

    unrolled(BI, fields)


def store_state(state, c, i, values):
    values = [turn(values[BJ - 1], 1, 1)] + values + [turn(values[0], -1, 1)]
    for j, value in enumerate(values):
        state[c, i + 1, j] = value
    if isinstance(i, int):
        for j, value in enumerate(values):
            if i == 0:
                state[c, BI + 1, j] = turn(value, -1, 0)
            else:
                state[c, 0, j] = turn(value, 1, 0)


def recip(x):
    y = pl.reciprocal(x, approx=True)
    y = y * (2.0 - x * y)
    return y * (2.0 - x * y)


def coefficients(spread, eta_spread, coef, weight, source, state, gx, gy, nx, ny):
    lane, sub = lanes(), sublanes()

    def row(i):
        r = gx * ROWS - HALO + BI * sub + i
        row_in = (r >= 0) & (r < nx)
        first, second = [], []
        for j in range(BJ):
            c = gy * COLS - HALO + BJ * (lane & 31) + j
            inside = row_in & (c >= 0) & (c < ny)
            m = eta_spread[i + 1, j + 1]
            e, w = eta_spread[i + 2, j + 1], eta_spread[i, j + 1]
            n, s = eta_spread[i + 1, j + 2], eta_spread[i + 1, j]
            react = spread[3, i, j] + DRAG
            me, mw, mn, ms = m + e, m + w, m + n, m + s
            along, across = me + mw, mn + ms
            w1 = jnp.where(inside, recip(2.0 * along + 0.5 * across + react), 0.0)
            w2 = jnp.where(inside, recip(0.5 * along + 2.0 * across + react), 0.0)
            a1, b1, q1 = 2.0 * w1, 0.5 * w1, 0.25 * w1
            a2, b2, q2 = 2.0 * w2, 0.5 * w2, 0.25 * w2
            coef[0, i, j] = a1 * me
            coef[1, i, j] = a1 * mw
            coef[2, i, j] = b1 * mn
            coef[3, i, j] = b1 * ms
            be, bw, qn, qs = b1 * e, b1 * w, q1 * n, q1 * s
            coef[4, i, j] = be + qn
            coef[5, i, j] = be + qs
            coef[6, i, j] = bw + qn
            coef[7, i, j] = bw + qs
            coef[8, i, j] = b2 * me
            coef[9, i, j] = b2 * mw
            coef[10, i, j] = a2 * mn
            coef[11, i, j] = a2 * ms
            bn, bs, qe, qw = b2 * n, b2 * s, q2 * e, q2 * w
            coef[12, i, j] = bn + qe
            coef[13, i, j] = bs + qe
            coef[14, i, j] = bn + qw
            coef[15, i, j] = bs + qw
            w1, w2 = OMEGA * w1, OMEGA * w2
            noise = spread[4, i, j]
            weight[0, i, j] = w1 * noise
            weight[1, i, j] = w2 * noise
            probe = spread[0, i, j]
            f1, f2 = w1 * (spread[1, i, j] * probe), w2 * (spread[2, i, j] * probe)
            source[0, i, j] = f1
            source[1, i, j] = f2
            first.append(SERIES[-1] * f1)
            second.append(SERIES[-1] * f2)
        store_state(state, 0, i, first)
        store_state(state, 1, i, second)

    ends_first(row)


def sweep(old, new, coef, source, factor):
    def row(i):
        first, second = [], []
        for j in range(BJ):

            def at(c, di, dj):
                return old[c, i + 1 + di, j + 1 + dj]

            k = [coef[n, i, j] for n in range(16)]
            first.append(
                factor * source[0, i, j]
                + (k[0] * at(0, 1, 0) + k[1] * at(0, -1, 0))
                + (k[2] * at(0, 0, 1) + k[3] * at(0, 0, -1))
                + (k[4] * at(1, 1, 1) - k[5] * at(1, 1, -1))
                + (k[7] * at(1, -1, -1) - k[6] * at(1, -1, 1))
            )
            second.append(
                factor * source[1, i, j]
                + (k[8] * at(1, 1, 0) + k[9] * at(1, -1, 0))
                + (k[10] * at(1, 0, 1) + k[11] * at(1, 0, -1))
                + (k[12] * at(0, 1, 1) - k[13] * at(0, 1, -1))
                + (k[15] * at(0, -1, -1) - k[14] * at(0, -1, 1))
            )
        store_state(new, 0, i, first)
        store_state(new, 1, i, second)

    ends_first(row)


def relax_twice(state_a, state_b, coef, source, between):

    def step(k, carry):
        for n in range(SWEEPS - 1):
            factor = SERIES[SWEEPS - 2 - n]
            old, new = (state_a, state_b) if n % 2 == 0 else (state_b, state_a)
            sweep(old, new, coef, source, factor)

        @pl.when(k == 0)
        def _():
            between()

        return carry

    lax.fori_loop(0, 2, step, 0)


def next_source(state, weight, source):
    def row(i):
        for c in range(2):
            values = [weight[c, i, j] * state[c, i + 1, j + 1] for j in range(BJ)]
            for j in range(BJ):
                source[c, i, j] = values[j]
            store_state(state, c, i, [SERIES[-1] * value for value in values])

    ends_first(row)


def gather_images(state, spread, natural):
    lane = lanes()
    place = lane + HALO
    block = (place * 205) >> 10
    rest = place - BJ * block

    def row(i):
        values = [
            spread[1, i, j] * state[0, i + 1, j + 1]
            + spread[2, i, j] * state[1, i + 1, j + 1]
            + PRIOR * spread[0, i, j]
            for j in range(BJ)
        ]
        for p in range(HALF):
            out = pick(values[0], block + 32 * p)
            for j in range(1, BJ):
                out = jnp.where(rest == j, pick(values[j], block + 32 * p), out)
            natural[p, pl.ds(i, 8, stride=BI), :] = out

    unrolled(BI, row)


def products(left, left_row, right, right_row):
    def add(k, totals):
        a = [left[p, pl.ds(left_row + 8 * k, 8), :] for p in range(HALF)]
        b = [right[p, pl.ds(right_row + 8 * k, 8), :] for p in range(HALF)]
        return tuple(t + a[n // 4] * b[n % 4] for n, t in enumerate(totals))

    zero = jnp.zeros((8, 128), F32)
    totals = lax.fori_loop(0, ROWS // 8, add, (zero,) * 16, unroll=True)
    sums = jnp.concatenate([jnp.sum(t, axis=0, keepdims=True) for t in totals], axis=0)
    sums = jnp.sum(sums, axis=1, keepdims=True)
    lane = lax.broadcasted_iota(jnp.int32, (16, 128), 1)
    row = lax.broadcasted_iota(jnp.int32, (16, 128), 0)
    return jnp.sum(jnp.where(lane == row, sums, 0.0), axis=0, keepdims=True)


def main_kernel(
    nx_devices, ny_devices,
    probes, velocity, eta_in, friction, noise, ice,
    images, other_images, gram,
    ext, west, east, left, right, eta, eta_west, eta_east, eta_left, eta_right,
    vel, fric, mask, side, eta_side, spread, eta_spread, coef, weight, source, state_a, state_b,
    natural, other_probes, message, inbox,
    in_sem, halo_send, halo_recv, eta_send, eta_recv, pair_send, pair_recv,
    sum_send, sum_recv, heard,
):
    half, gx, gy = lax.axis_index("probe"), lax.axis_index("gx"), lax.axis_index("gy")
    own_rows = slice(HALO, HALO + ROWS)

    loads = [
        pltpu.make_async_copy(velocity, vel, in_sem.at[0]),
        pltpu.make_async_copy(friction, fric, in_sem.at[1]),
        pltpu.make_async_copy(ice, mask, in_sem.at[2]),
        pltpu.make_async_copy(probes, ext.at[0:HALF, own_rows, :], in_sem.at[3]),
        pltpu.make_async_copy(noise, ext.at[7, own_rows, :], in_sem.at[4]),
        pltpu.make_async_copy(eta_in, eta.at[ETA_HALO : ETA_HALO + ROWS, :], in_sem.at[5]),
    ]
    for load in loads:
        load.start()

    def blank(ref):
        ref[...] = jnp.zeros(ref.shape, F32)

    @pl.when(gx == 0)
    def _():
        blank(ext.at[:, 0:HALO, :])
        blank(eta.at[0:ETA_HALO, :])
        for ref in (west, east):
            blank(ref.at[0:HALO, :])
        for ref in (eta_west, eta_east):
            blank(ref.at[0])

    @pl.when(gx == nx_devices - 1)
    def _():
        blank(ext.at[:, HALO + ROWS : EXT, :])
        blank(eta.at[ETA_HALO + ROWS : 2 * ETA_HALO + ROWS, :])
        for ref in (west, east):
            blank(ref.at[HALO + ROWS : EXT, :])
        for ref in (eta_west, eta_east):
            blank(ref.at[2])

    @pl.when(gy == 0)
    def _():
        blank(west)
        blank(eta_west)

    @pl.when(gy == ny_devices - 1)
    def _():
        blank(east)
        blank(eta_east)

    def exists(dx, dy):
        x, y = gx + dx, gy + dy
        return (x >= 0) & (x < nx_devices) & (y >= 0) & (y < ny_devices)

    def away(dx, dy):
        return {"gx": lax.rem(gx + dx + nx_devices, nx_devices), "gy": lax.rem(gy + dy + ny_devices, ny_devices)}

    partner = {"probe": 1 - half}

    def signal(semaphore, to):
        pl.semaphore_signal(semaphore, inc=1, device_id=to, device_id_type=MESH)

    barrier = pltpu.get_barrier_semaphore()
    for dx, dy in AROUND:
        signal(barrier, away(dx, dy))
    signal(barrier, partner)

    relays = (AROUND, [(2 * dx, 2 * dy) for dx, dy in AROUND], [(-4, 0), (4, 0)], [])

    def relay(stage):
        for dx, dy in relays[stage]:
            signal(heard.at[stage], away(dx, dy))
        signal(heard.at[stage], partner)

    def hear(stage):
        pl.semaphore_wait(heard.at[stage], len(relays[stage]) + 1)

    for load in loads:
        load.wait()
    coupling = fric[...] * mask[...].astype(F32)
    ext[4, own_rows, :] = -coupling * vel[0]
    ext[5, own_rows, :] = -coupling * vel[1]
    ext[6, own_rows, :] = coupling
    pack_strips(ext, eta, left, right, eta_left, eta_right)

    pl.semaphore_wait(barrier, len(AROUND) + 1)

    def halo_copies(n):
        dx, dy = AROUND[n]
        to = {"gx": gx + dx, "gy": gy + dy}
        if dy == 0:
            src_row, dst_row = (ROWS, 0) if dx > 0 else (HALO, HALO + ROWS)
            main = (ext.at[:, src_row : src_row + HALO, :], ext.at[:, dst_row : dst_row + HALO, :])
            src_row, dst_row = (ROWS, 0) if dx > 0 else (ETA_HALO, ETA_HALO + ROWS)
            more = (eta.at[src_row : src_row + ETA_HALO, :], eta.at[dst_row : dst_row + ETA_HALO, :])
        else:
            strip, landing = (right, west) if dy > 0 else (left, east)
            src_row, dst_row, count = {0: (0, HALO, ROWS), 1: (ROWS - HALO, 0, HALO), -1: (0, HALO + ROWS, HALO)}[dx]
            main = (strip.at[src_row : src_row + count, :], landing.at[dst_row : dst_row + count, :])
            strip, landing = (eta_right, eta_west) if dy > 0 else (eta_left, eta_east)
            more = (strip, landing.at[1 - dx])
        return [
            pltpu.make_async_remote_copy(
                src_ref=src, dst_ref=dst, send_sem=sends.at[n], recv_sem=recvs.at[n], device_id=to, device_id_type=MESH
            )
            for (src, dst), sends, recvs in ((main, halo_send, halo_recv), (more, eta_send, eta_recv))
        ]

    for n, (dx, dy) in reversed(list(enumerate(AROUND))):

        @pl.when(exists(dx, dy))
        def _():
            for copy in halo_copies(n):
                copy.start()

    relay(0)

    probe_copy = pltpu.make_async_remote_copy(
        src_ref=ext.at[0:HALF, own_rows, :], dst_ref=other_probes,
        send_sem=pair_send.at[0], recv_sem=pair_recv.at[0], device_id={"probe": 1 - half}, device_id_type=MESH,
    )
    image_copy = pltpu.make_async_remote_copy(
        src_ref=natural.at[:, own_rows, :], dst_ref=other_images,
        send_sem=pair_send.at[1], recv_sem=pair_recv.at[1], device_id={"probe": 1 - half}, device_id_type=MESH,
    )

    def await_halos(directions):
        for n in directions:
            dx, dy = AROUND[n]

            @pl.when(exists(-dx, -dy))
            def _():
                for copy in halo_copies(n):
                    copy.wait_recv()

    await_halos((0, 1))
    relayout_own(ext, eta, spread, eta_spread)
    hear(0)
    relay(1)
    await_halos(range(2, 8))

    @pl.when(half == 1)
    def _():
        probe_copy.start()

    relayout_sides(west, east, eta_west, eta_east, side, eta_side, spread, eta_spread)
    coefficients(
        spread, eta_spread, coef, weight, source, state_a, gx, gy, nx_devices * ROWS, ny_devices * COLS
    )
    hear(1)
    relay(2)

    def between():
        next_source(state_a, weight, source)
        hear(2)
        relay(3)

    relax_twice(state_a, state_b, coef, source, between)
    gather_images(state_a, spread, natural)

    @pl.when(half == 0)
    def _():
        image_copy.start()

    hear(3)
    own = products(ext, HALO, natural, HALO)

    @pl.when(half == 0)
    def _():
        probe_copy.wait_recv()
        cross = products(other_probes, 0, natural, HALO)
        message[0] = own + turn(cross, 16, 1)

    @pl.when(half == 1)
    def _():
        message[0] = turn(own, 32, 1)

    me = (gx * ny_devices + gy) * 2 + half
    everyone = 2 * nx_devices * ny_devices

    def sum_copy(dx, dy, dp, to_all):
        to = {
            "gx": lax.rem(gx + dx, nx_devices),
            "gy": lax.rem(gy + dy, ny_devices),
            "probe": lax.rem(half + dp, 2),
        }
        rows = everyone - 1 if to_all else 1
        src = inbox.at[0:rows] if to_all else message
        dst = inbox.at[0:rows] if to_all else inbox.at[pl.ds(me, 1)]
        return pltpu.make_async_remote_copy(
            src_ref=src, dst_ref=dst, send_sem=sum_send, recv_sem=sum_recv, device_id=to, device_id_type=MESH
        )

    y_order = (4, 3, 5, 2, 6, 1, 7, 0)

    def send_sums(k, carry):
        step = lax.div(k + 1, 2)
        dx = lax.rem(nx_devices // 2 + nx_devices + jnp.where(lax.rem(k, 2) == 0, step, -step), nx_devices)
        for dy in y_order:
            for dp in (1, 0):
                if dy == 0 and dp == 0:

                    @pl.when(dx != 0)
                    def _():
                        sum_copy(dx, dy, dp, False).start()
                else:
                    sum_copy(dx, dy, dp, False).start()
        return carry

    lax.fori_loop(0, nx_devices, send_sums, 0)
    inbox[pl.ds(me, 1)] = message[...]
    images[...] = natural[:, own_rows, :]
    all_sums = sum_copy(1, 0, 0, True)
    all_sums.wait_recv()
    total = jnp.sum(jnp.sum(inbox[...].reshape(everyone // 8, 8, 128), axis=0), axis=0, keepdims=True)
    gram[...] = jnp.broadcast_to(total * (1.0 / (nx_devices * ROWS * ny_devices * COLS)), (8, 128))

    for n, (dx, dy) in enumerate(AROUND):

        @pl.when(exists(dx, dy))
        def _():
            for copy in halo_copies(n):
                copy.wait_send()

    all_sums.wait_send()

    @pl.when(half == 0)
    def _():
        image_copy.wait_send()

    @pl.when(half == 1)
    def _():
        probe_copy.wait_send()
        image_copy.wait_recv()


def last_kernel(sums, images, other_images, images_out, factor, gram, factor_here, gram_here, sems):
    half = lax.axis_index("probe")
    images_copy = pltpu.make_async_copy(images, images_out, sems.at[0])
    images_copy.start()

    lane, sub = lanes(), sublanes()
    low_row, low_col = sub < HALF, lane < HALF
    a, b = sub & (HALF - 1), lane & (HALF - 1)
    at = jnp.where(low_row == low_col, HALF * a + b, jnp.where(low_col, HALF * a + b, HALF * b + a))
    at = at + jnp.where(low_row == low_col, jnp.where(low_row, 0, 2 * HALF * HALF), HALF * HALF)
    row = sums[...]
    full = pick(row, jnp.where(lane < 2 * HALF, at, 0))
    gram_here[...] = full[:, : 2 * HALF]
    gram_copy = pltpu.make_async_copy(gram_here, gram, sems.at[1])
    gram_copy.start()

    def entry(i, j):
        k = HALF * (i % HALF) + j % HALF
        if (i < HALF) == (j < HALF):
            return jnp.broadcast_to(row[:, (k if i < HALF else k + 32) :][:, :1], (8, 128))
        return jnp.broadcast_to(row[:, k + 16 :][:, :1], (8, 128))

    count = 2 * HALF
    low, inverse = {}, {}
    for j in range(count):
        for i in range(j, count):
            value = entry(i, j)
            if i != j and (i < HALF) == (j < HALF):
                value = 0.5 * (value + entry(j, i))
            for k in range(j):
                value = value - low[i, k] * low[j, k]
            if i == j:
                guess = lax.rsqrt(value)
                inverse[j] = guess * (1.5 - 0.5 * value * guess * guess)
            else:
                low[i, j] = value * inverse[j]

    def solve(sources):
        def part(k):
            rows = pl.ds(8 * k, 8)
            done = []
            for i, (ref, p) in enumerate(sources):
                value = ref[p, rows, :]
                for j in range(i):
                    value = value - low[i, j] * done[j]
                value = value * inverse[i]
                done.append(value)
                if i >= len(sources) - HALF:
                    factor_here[i - len(sources) + HALF, rows, :] = value

        unrolled(ROWS // 8, part)

    @pl.when(half == 0)
    def _():
        solve([(images, p) for p in range(HALF)])

    @pl.when(half == 1)
    def _():
        solve([(other_images, p) for p in range(HALF)] + [(images, p) for p in range(HALF)])

    factor_copy = pltpu.make_async_copy(factor_here, factor, sems.at[2])
    factor_copy.start()
    images_copy.wait()
    gram_copy.wait()
    factor_copy.wait()


def body(probes, velocity, eta, friction, noise, ice):
    nx_devices, ny_devices = lax.axis_size("gx"), lax.axis_size("gy")
    vmem = lambda *shape: pltpu.VMEM(shape, F32)
    dma = lambda count: pltpu.SemaphoreType.DMA((count,))
    grid = (BI, BJ, 8, 128)
    padded = (BI + 2, BJ + 2, 8, 128)
    whole = pl.BlockSpec(memory_space=pltpu.VMEM)
    tile = jax.ShapeDtypeStruct((HALF, ROWS, COLS), F32)
    images, other_images, sums = pl.pallas_call(
        functools.partial(main_kernel, nx_devices, ny_devices),
        out_shape=(tile, tile, jax.ShapeDtypeStruct((8, 128), F32)),
        in_specs=[pl.BlockSpec(memory_space=pl.ANY)] * 6,
        out_specs=(whole, whole, whole),
        scratch_shapes=[
            vmem(8, EXT, 128), vmem(EXT, 128), vmem(EXT, 128), vmem(ROWS, 128), vmem(ROWS, 128),
            vmem(ROWS + 2 * ETA_HALO, 128), vmem(3, 16, 128), vmem(3, 16, 128), vmem(16, 128), vmem(16, 128),
            vmem(2, ROWS, COLS), vmem(ROWS, COLS), pltpu.VMEM((ROWS, COLS), jnp.int32),
            vmem(2, EXT, 128), vmem(ROWS + 2 * ETA_HALO, 128),
            vmem(5, *grid), vmem(*padded), vmem(16, *grid), vmem(2, *grid), vmem(2, *grid),
            vmem(2, *padded), vmem(2, *padded),
            vmem(HALF, EXT, 128), vmem(HALF, ROWS, COLS), vmem(1, 1, 128), vmem(2 * nx_devices * ny_devices, 1, 128),
            dma(6), dma(8), dma(8), dma(8), dma(8), dma(2), dma(2),
            pltpu.SemaphoreType.DMA, pltpu.SemaphoreType.DMA,
            pltpu.SemaphoreType.REGULAR((4,)),
        ],
        compiler_params=pltpu.CompilerParams(
            collective_id=0, has_side_effects=True, vmem_limit_bytes=32 * 1024 * 1024
        ),
    )(*[pltpu.with_memory_space_constraint(x, pltpu.HBM) for x in (probes, velocity, eta, friction, noise, ice)])
    square = (2 * HALF, 2 * HALF)
    return pl.pallas_call(
        last_kernel,
        out_shape=(tile, tile, jax.ShapeDtypeStruct(square, F32)),
        in_specs=[whole, whole, whole],
        out_specs=(pl.BlockSpec(memory_space=pl.ANY),) * 3,
        scratch_shapes=[vmem(HALF, ROWS, COLS), vmem(*square), dma(3)],
        compiler_params=pltpu.CompilerParams(vmem_limit_bytes=16 * 1024 * 1024),
    )(sums, images, other_images)


def solution(mesh):
    in_specs = (
        P("probe", "gx", "gy"),
        P(None, "gx", "gy"),
        P("gx", "gy"),
        P("gx", "gy"),
        P("gx", "gy"),
        P("gx", "gy"),
    )
    out_specs = (P("probe", "gx", "gy"), P("probe", "gx", "gy"), P())
    return jax.shard_map(body, mesh=mesh, in_specs=in_specs, out_specs=out_specs, check_vma=False)
```

```python
import functools

import jax
import jax.numpy as jnp
import numpy as np
from jax import lax
from jax.experimental import pallas as pl
from jax.experimental.pallas import tpu as pltpu
from jax.sharding import PartitionSpec as P

SWEEPS = 9
OMEGA = 0.6
DRAG = 0.05
PRIOR = 0.05

HALF = 4
ROWS, COLS = 64, 128
HALO = 2 * (SWEEPS - 1)
BI, BJ = (ROWS + 2 * HALO) // 8, (COLS + 2 * HALO) // 32
EXT = ROWS + 2 * HALO
ROOM = 16
ETA_HALO = 24
MESH = pl.DeviceIdType.MESH
F32 = jnp.float32
SERIES = np.polynomial.Polynomial([0.0])
for power in range(SWEEPS):
    SERIES = SERIES + np.polynomial.Polynomial([1.0 - OMEGA, OMEGA]) ** power
SERIES = [float(a) for a in SERIES.coef]
AROUND = ((-1, 0), (1, 0), (0, -1), (0, 1), (-1, -1), (-1, 1), (1, -1), (1, 1))


def lanes():
    return lax.broadcasted_iota(jnp.int32, (8, 128), 1)


def sublanes():
    return lax.broadcasted_iota(jnp.int32, (8, 128), 0)


def turn(x, shift, axis):
    shift = shift % x.shape[axis]
    return pltpu.roll(x, shift, axis) if shift else x


def pick(x, index):
    return jnp.take_along_axis(x, index, axis=1, mode="promise_in_bounds")


def unrolled(count, body, start=0):
    def step(i, carry):
        body(i)
        return carry

    lax.fori_loop(start, count, step, 0, unroll=True)


def ends_first(body):
    body(0)
    body(BI - 1)
    unrolled(BI - 1, body, 1)


def pack_strips(ext, eta, left, right, eta_left, eta_right):
    lane = lax.broadcasted_iota(jnp.int32, (ROWS, COLS), 1)
    for f in range(8):
        own = ext[f, HALO : HALO + ROWS, :]
        here = (lane >= 16 * f) & (lane < 16 * f + 16)
        first, last = turn(own, 16 * f, 1), turn(own, 16 * f + 16, 1)
        left[...] = first if f == 0 else jnp.where(here, first, left[...])
        right[...] = last if f == 0 else jnp.where(here, last, right[...])
    lane = lax.broadcasted_iota(jnp.int32, (16, COLS), 1)
    first = last = None
    for g in range(4):
        own = eta[ETA_HALO + 16 * g : ETA_HALO + 16 * g + 16, :]
        here = (lane >= 32 * g) & (lane < 32 * g + 32)
        a, b = turn(own, 32 * g, 1), turn(own, 32 * g + 32, 1)
        first = a if g == 0 else jnp.where(here, a, first)
        last = b if g == 0 else jnp.where(here, b, last)
    eta_left[...] = first
    eta_right[...] = last


def places(j):
    col = BJ * (lanes() & 31) + j - HALO
    return col, jnp.clip(col, 0, COLS - 1), (col < 0) | (col >= COLS)


def relayout_own(ext, eta, spread, eta_spread):
    group = lanes() >> 5

    def fields(i):
        rows = pl.ds(i, 8, stride=BI)
        own = [ext[f, rows, :] for f in range(8)]
        for j in range(BJ):
            _, at, _ = places(j)
            value = pick(own[HALF - 1], at)
            for p in range(HALF - 2, -1, -1):
                value = jnp.where(group == p, pick(own[p], at), value)
            spread[0, i, j] = value
            for f in range(4):
                spread[1 + f, i, j] = pick(own[4 + f], at)

    unrolled(BI, fields)

    def viscosity(i):
        own = eta[pl.ds(i + ETA_HALO - HALO - 1, 8, stride=BI), :]
        for j in range(-1, BJ + 1):
            eta_spread[i, j + 1] = pick(own, places(j)[1])

    unrolled(BI + 2, viscosity)


def relayout_sides(west, east, eta_west, eta_east, side, eta_side, spread, eta_spread):
    lane = lanes()
    group = lane >> 5
    wide = lax.broadcasted_iota(jnp.int32, (EXT, COLS), 1)
    w, e = west[...], east[...]
    side[0, 0:EXT, :] = jnp.where(wide < 64, w, turn(e, 64, 1))
    side[1, 0:EXT, :] = jnp.where(wide < 64, turn(w, 64, 1), e)
    for k in range(14):
        own_row = 8 * k - ETA_HALO
        slot = 0 if own_row < 0 else (1 if own_row < ROWS else 2)
        row = own_row - ROWS * (slot - 1)
        g, r = row // 16, row % 16
        a = turn(eta_west[slot, r : r + 8, :], -32 * g, 1)
        b = turn(eta_east[slot, r : r + 8, :], 32 - 32 * g, 1)
        eta_side[8 * k : 8 * k + 8, :] = jnp.where(lane < 32, a, b)

    def viscosity(i):
        beside = eta_side[pl.ds(i + ETA_HALO - HALO - 1, 8, stride=BI), :]
        for j in range(-1, BJ + 1):
            col, _, outside = places(j)
            at = jnp.where(outside, jnp.where(col < 0, col + 32, col - COLS + 32), 0)
            eta_spread[i, j + 1] = jnp.where(outside, pick(beside, at), eta_spread[i, j + 1])

    unrolled(BI + 2, viscosity)

    def fields(i):
        rows = pl.ds(i, 8, stride=BI)
        low, high = side[0, rows, :], side[1, rows, :]
        for j in range(BJ):
            col, _, outside = places(j)
            at = jnp.where(outside, jnp.where(col < 0, col + HALO, col - COLS + 64), 0)
            spread[0, i, j] = jnp.where(outside, pick(low, at + 16 * group), spread[0, i, j])
            for f in range(4):
                spread[1 + f, i, j] = jnp.where(outside, pick(high, at + 16 * f), spread[1 + f, i, j])

    unrolled(BI, fields)


def store_state(state, c, i, values):
    values = [turn(values[BJ - 1], 1, 1)] + values + [turn(values[0], -1, 1)]
    for j, value in enumerate(values):
        state[c, i + 1, j] = value
    if isinstance(i, int):
        for j, value in enumerate(values):
            if i == 0:
                state[c, BI + 1, j] = turn(value, -1, 0)
            else:
                state[c, 0, j] = turn(value, 1, 0)


def recip(x):
    y = pl.reciprocal(x, approx=True)
    y = y * (2.0 - x * y)
    return y * (2.0 - x * y)


def coefficients(spread, eta_spread, coef, weight, source, state, gx, gy, nx, ny):
    lane, sub = lanes(), sublanes()

    def row(i):
        r = gx * ROWS - HALO + BI * sub + i
        row_in = (r >= 0) & (r < nx)
        first, second = [], []
        for j in range(BJ):
            c = gy * COLS - HALO + BJ * (lane & 31) + j
            inside = row_in & (c >= 0) & (c < ny)
            m = eta_spread[i + 1, j + 1]
            e, w = eta_spread[i + 2, j + 1], eta_spread[i, j + 1]
            n, s = eta_spread[i + 1, j + 2], eta_spread[i + 1, j]
            react = spread[3, i, j] + DRAG
            me, mw, mn, ms = m + e, m + w, m + n, m + s
            along, across = me + mw, mn + ms
            w1 = jnp.where(inside, recip(2.0 * along + 0.5 * across + react), 0.0)
            w2 = jnp.where(inside, recip(0.5 * along + 2.0 * across + react), 0.0)
            a1, b1, q1 = 2.0 * w1, 0.5 * w1, 0.25 * w1
            a2, b2, q2 = 2.0 * w2, 0.5 * w2, 0.25 * w2
            coef[0, i, j] = a1 * me
            coef[1, i, j] = a1 * mw
            coef[2, i, j] = b1 * mn
            coef[3, i, j] = b1 * ms
            be, bw, qn, qs = b1 * e, b1 * w, q1 * n, q1 * s
            coef[4, i, j] = be + qn
            coef[5, i, j] = be + qs
            coef[6, i, j] = bw + qn
            coef[7, i, j] = bw + qs
            coef[8, i, j] = b2 * me
            coef[9, i, j] = b2 * mw
            coef[10, i, j] = a2 * mn
            coef[11, i, j] = a2 * ms
            bn, bs, qe, qw = b2 * n, b2 * s, q2 * e, q2 * w
            coef[12, i, j] = bn + qe
            coef[13, i, j] = bs + qe
            coef[14, i, j] = bn + qw
            coef[15, i, j] = bs + qw
            w1, w2 = OMEGA * w1, OMEGA * w2
            noise = spread[4, i, j]
            weight[0, i, j] = w1 * noise
            weight[1, i, j] = w2 * noise
            probe = spread[0, i, j]
            f1, f2 = w1 * (spread[1, i, j] * probe), w2 * (spread[2, i, j] * probe)
            source[0, i, j] = f1
            source[1, i, j] = f2
            first.append(SERIES[-1] * f1)
            second.append(SERIES[-1] * f2)
        store_state(state, 0, i, first)
        store_state(state, 1, i, second)

    ends_first(row)


def sweep(old, new, coef, source, factor):
    def row(i):
        first, second = [], []
        for j in range(BJ):

            def at(c, di, dj):
                return old[c, i + 1 + di, j + 1 + dj]

            k = [coef[n, i, j] for n in range(16)]
            first.append(
                factor * source[0, i, j]
                + (k[0] * at(0, 1, 0) + k[1] * at(0, -1, 0))
                + (k[2] * at(0, 0, 1) + k[3] * at(0, 0, -1))
                + (k[4] * at(1, 1, 1) - k[5] * at(1, 1, -1))
                + (k[7] * at(1, -1, -1) - k[6] * at(1, -1, 1))
            )
            second.append(
                factor * source[1, i, j]
                + (k[8] * at(1, 1, 0) + k[9] * at(1, -1, 0))
                + (k[10] * at(1, 0, 1) + k[11] * at(1, 0, -1))
                + (k[12] * at(0, 1, 1) - k[13] * at(0, 1, -1))
                + (k[15] * at(0, -1, -1) - k[14] * at(0, -1, 1))
            )
        store_state(new, 0, i, first)
        store_state(new, 1, i, second)

    ends_first(row)


def relax_twice(state_a, state_b, coef, source, between):

    def step(k, carry):
        for n in range(SWEEPS - 1):
            factor = SERIES[SWEEPS - 2 - n]
            old, new = (state_a, state_b) if n % 2 == 0 else (state_b, state_a)
            sweep(old, new, coef, source, factor)

        @pl.when(k == 0)
        def _():
            between()

        return carry

    lax.fori_loop(0, 2, step, 0)


def next_source(state, weight, source):
    def row(i):
        for c in range(2):
            values = [weight[c, i, j] * state[c, i + 1, j + 1] for j in range(BJ)]
            for j in range(BJ):
                source[c, i, j] = values[j]
            store_state(state, c, i, [SERIES[-1] * value for value in values])

    ends_first(row)


def gather_images(state, spread, natural):
    lane = lanes()
    place = lane + HALO
    block = (place * 205) >> 10
    rest = place - BJ * block

    def row(i):
        values = [
            spread[1, i, j] * state[0, i + 1, j + 1]
            + spread[2, i, j] * state[1, i + 1, j + 1]
            + PRIOR * spread[0, i, j]
            for j in range(BJ)
        ]
        for p in range(HALF):
            out = pick(values[0], block + 32 * p)
            for j in range(1, BJ):
                out = jnp.where(rest == j, pick(values[j], block + 32 * p), out)
            natural[p, pl.ds(i, 8, stride=BI), :] = out

    unrolled(BI, row)


def products(left, left_row, right, right_row):
    def add(k, totals):
        a = [left[p, pl.ds(left_row + 8 * k, 8), :] for p in range(HALF)]
        b = [right[p, pl.ds(right_row + 8 * k, 8), :] for p in range(HALF)]
        return tuple(t + a[n // 4] * b[n % 4] for n, t in enumerate(totals))

    zero = jnp.zeros((8, 128), F32)
    totals = lax.fori_loop(0, ROWS // 8, add, (zero,) * 16, unroll=True)
    sums = jnp.concatenate([jnp.sum(t, axis=0, keepdims=True) for t in totals], axis=0)
    sums = jnp.sum(sums, axis=1, keepdims=True)
    lane = lax.broadcasted_iota(jnp.int32, (16, 128), 1)
    row = lax.broadcasted_iota(jnp.int32, (16, 128), 0)
    return jnp.sum(jnp.where(lane == row, sums, 0.0), axis=0, keepdims=True)


def main_kernel(
    nx_devices, ny_devices,
    probes, velocity, eta_in, friction, noise, ice,
    images, other_images, gram,
    ext, west, east, left, right, eta, eta_west, eta_east, eta_left, eta_right,
    vel, fric, mask, side, eta_side, spread, eta_spread, coef, weight, source, state_a, state_b,
    natural, other_probes, message, inbox,
    in_sem, halo_send, halo_recv, eta_send, eta_recv, pair_send, pair_recv,
    sum_send, sum_recv, heard,
):
    half, gx, gy = lax.axis_index("probe"), lax.axis_index("gx"), lax.axis_index("gy")
    own_rows = slice(HALO, HALO + ROWS)

    loads = [
        pltpu.make_async_copy(velocity, vel, in_sem.at[0]),
        pltpu.make_async_copy(friction, fric, in_sem.at[1]),
        pltpu.make_async_copy(ice, mask, in_sem.at[2]),
        pltpu.make_async_copy(probes, ext.at[0:HALF, own_rows, :], in_sem.at[3]),
        pltpu.make_async_copy(noise, ext.at[7, own_rows, :], in_sem.at[4]),
        pltpu.make_async_copy(eta_in, eta.at[ETA_HALO : ETA_HALO + ROWS, :], in_sem.at[5]),
    ]
    for load in loads:
        load.start()

    def blank(ref):
        ref[...] = jnp.zeros(ref.shape, F32)

    @pl.when(gx == 0)
    def _():
        blank(ext.at[:, 0:HALO, :])
        blank(eta.at[0:ETA_HALO, :])
        for ref in (west, east):
            blank(ref.at[0:HALO, :])
        for ref in (eta_west, eta_east):
            blank(ref.at[0])

    @pl.when(gx == nx_devices - 1)
    def _():
        blank(ext.at[:, HALO + ROWS : EXT, :])
        blank(eta.at[ETA_HALO + ROWS : 2 * ETA_HALO + ROWS, :])
        for ref in (west, east):
            blank(ref.at[HALO + ROWS : EXT, :])
        for ref in (eta_west, eta_east):
            blank(ref.at[2])

    @pl.when(gy == 0)
    def _():
        blank(west)
        blank(eta_west)

    @pl.when(gy == ny_devices - 1)
    def _():
        blank(east)
        blank(eta_east)

    def exists(dx, dy):
        x, y = gx + dx, gy + dy
        return (x >= 0) & (x < nx_devices) & (y >= 0) & (y < ny_devices)

    def away(dx, dy):
        return {"gx": lax.rem(gx + dx + nx_devices, nx_devices), "gy": lax.rem(gy + dy + ny_devices, ny_devices)}

    partner = {"probe": 1 - half}

    def signal(semaphore, to):
        pl.semaphore_signal(semaphore, inc=1, device_id=to, device_id_type=MESH)

    barrier = pltpu.get_barrier_semaphore()
    for dx, dy in AROUND:
        signal(barrier, away(dx, dy))
    signal(barrier, partner)

    relays = (AROUND, [(2 * dx, 2 * dy) for dx, dy in AROUND], [(-4, 0), (4, 0)], [])

    def relay(stage):
        for dx, dy in relays[stage]:
            signal(heard.at[stage], away(dx, dy))
        signal(heard.at[stage], partner)

    def hear(stage):
        pl.semaphore_wait(heard.at[stage], len(relays[stage]) + 1)

    for load in loads:
        load.wait()
    coupling = fric[...] * mask[...].astype(F32)
    ext[4, own_rows, :] = -coupling * vel[0]
    ext[5, own_rows, :] = -coupling * vel[1]
    ext[6, own_rows, :] = coupling
    pack_strips(ext, eta, left, right, eta_left, eta_right)

    pl.semaphore_wait(barrier, len(AROUND) + 1)

    def halo_copies(n):
        dx, dy = AROUND[n]
        to = {"gx": gx + dx, "gy": gy + dy}
        if dy == 0:
            src_row, dst_row = (ROWS, 0) if dx > 0 else (HALO, HALO + ROWS)
            main = (ext.at[:, src_row : src_row + HALO, :], ext.at[:, dst_row : dst_row + HALO, :])
            src_row, dst_row = (ROWS, 0) if dx > 0 else (ETA_HALO, ETA_HALO + ROWS)
            more = (eta.at[src_row : src_row + ETA_HALO, :], eta.at[dst_row : dst_row + ETA_HALO, :])
        else:
            strip, landing = (right, west) if dy > 0 else (left, east)
            src_row, dst_row, count = {0: (0, HALO, ROWS), 1: (ROWS - HALO, 0, HALO), -1: (0, HALO + ROWS, HALO)}[dx]
            main = (strip.at[src_row : src_row + count, :], landing.at[dst_row : dst_row + count, :])
            strip, landing = (eta_right, eta_west) if dy > 0 else (eta_left, eta_east)
            more = (strip, landing.at[1 - dx])
        return [
            pltpu.make_async_remote_copy(
                src_ref=src, dst_ref=dst, send_sem=sends.at[n], recv_sem=recvs.at[n], device_id=to, device_id_type=MESH
            )
            for (src, dst), sends, recvs in ((main, halo_send, halo_recv), (more, eta_send, eta_recv))
        ]

    for n, (dx, dy) in reversed(list(enumerate(AROUND))):

        @pl.when(exists(dx, dy))
        def _():
            for copy in halo_copies(n):
                copy.start()

    relay(0)

    probe_copy = pltpu.make_async_remote_copy(
        src_ref=ext.at[0:HALF, own_rows, :], dst_ref=other_probes,
        send_sem=pair_send.at[0], recv_sem=pair_recv.at[0], device_id={"probe": 1 - half}, device_id_type=MESH,
    )
    image_copy = pltpu.make_async_remote_copy(
        src_ref=natural.at[:, own_rows, :], dst_ref=other_images,
        send_sem=pair_send.at[1], recv_sem=pair_recv.at[1], device_id={"probe": 1 - half}, device_id_type=MESH,
    )

    def await_halos(directions):
        for n in directions:
            dx, dy = AROUND[n]

            @pl.when(exists(-dx, -dy))
            def _():
                for copy in halo_copies(n):
                    copy.wait_recv()

    await_halos((0, 1))
    relayout_own(ext, eta, spread, eta_spread)
    hear(0)
    relay(1)
    await_halos(range(2, 8))

    @pl.when(half == 1)
    def _():
        probe_copy.start()

    relayout_sides(west, east, eta_west, eta_east, side, eta_side, spread, eta_spread)
    coefficients(
        spread, eta_spread, coef, weight, source, state_a, gx, gy, nx_devices * ROWS, ny_devices * COLS
    )
    hear(1)
    relay(2)

    def between():
        next_source(state_a, weight, source)
        hear(2)
        relay(3)

    relax_twice(state_a, state_b, coef, source, between)
    gather_images(state_a, spread, natural)

    @pl.when(half == 0)
    def _():
        image_copy.start()

    hear(3)
    own = products(ext, HALO, natural, HALO)

    @pl.when(half == 0)
    def _():
        probe_copy.wait_recv()
        cross = products(other_probes, 0, natural, HALO)
        message[0] = own + turn(cross, 16, 1)

    @pl.when(half == 1)
    def _():
        message[0] = turn(own, 32, 1)

    me = (gx * ny_devices + gy) * 2 + half
    everyone = 2 * nx_devices * ny_devices

    def sum_copy(dx, dy, dp, to_all):
        to = {
            "gx": lax.rem(gx + dx, nx_devices),
            "gy": lax.rem(gy + dy, ny_devices),
            "probe": lax.rem(half + dp, 2),
        }
        rows = everyone - 1 if to_all else 1
        src = inbox.at[0:rows] if to_all else message
        dst = inbox.at[0:rows] if to_all else inbox.at[pl.ds(me, 1)]
        return pltpu.make_async_remote_copy(
            src_ref=src, dst_ref=dst, send_sem=sum_send, recv_sem=sum_recv, device_id=to, device_id_type=MESH
        )

    y_order = (4, 3, 5, 2, 6, 1, 7, 0)

    def send_sums(k, carry):
        step = lax.div(k + 1, 2)
        dx = lax.rem(nx_devices // 2 + nx_devices + jnp.where(lax.rem(k, 2) == 0, step, -step), nx_devices)
        for dy in y_order:
            for dp in (1, 0):
                if dy == 0 and dp == 0:

                    @pl.when(dx != 0)
                    def _():
                        sum_copy(dx, dy, dp, False).start()
                else:
                    sum_copy(dx, dy, dp, False).start()
        return carry

    lax.fori_loop(0, nx_devices, send_sums, 0)
    inbox[pl.ds(me, 1)] = message[...]
    images[...] = natural[:, own_rows, :]
    all_sums = sum_copy(1, 0, 0, True)
    all_sums.wait_recv()
    total = jnp.sum(jnp.sum(inbox[...].reshape(everyone // 8, 8, 128), axis=0), axis=0, keepdims=True)
    gram[...] = jnp.broadcast_to(total * (1.0 / (nx_devices * ROWS * ny_devices * COLS)), (8, 128))

    for n, (dx, dy) in enumerate(AROUND):

        @pl.when(exists(dx, dy))
        def _():
            for copy in halo_copies(n):
                copy.wait_send()

    all_sums.wait_send()

    @pl.when(half == 0)
    def _():
        image_copy.wait_send()

    @pl.when(half == 1)
    def _():
        probe_copy.wait_send()
        image_copy.wait_recv()


def last_kernel(sums, images, other_images, images_out, factor, gram, factor_here, gram_here, sems):
    half = lax.axis_index("probe")
    images_copy = pltpu.make_async_copy(images, images_out, sems.at[0])
    images_copy.start()

    lane, sub = lanes(), sublanes()
    low_row, low_col = sub < HALF, lane < HALF
    a, b = sub & (HALF - 1), lane & (HALF - 1)
    at = jnp.where(low_row == low_col, HALF * a + b, jnp.where(low_col, HALF * a + b, HALF * b + a))
    at = at + jnp.where(low_row == low_col, jnp.where(low_row, 0, 2 * HALF * HALF), HALF * HALF)
    row = sums[...]
    full = pick(row, jnp.where(lane < 2 * HALF, at, 0))
    gram_here[...] = full[:, : 2 * HALF]
    gram_copy = pltpu.make_async_copy(gram_here, gram, sems.at[1])
    gram_copy.start()

    def entry(i, j):
        k = HALF * (i % HALF) + j % HALF
        if (i < HALF) == (j < HALF):
            return jnp.broadcast_to(row[:, (k if i < HALF else k + 32) :][:, :1], (8, 128))
        return jnp.broadcast_to(row[:, k + 16 :][:, :1], (8, 128))

    count = 2 * HALF
    low, inverse = {}, {}
    for j in range(count):
        for i in range(j, count):
            value = entry(i, j)
            if i != j and (i < HALF) == (j < HALF):
                value = 0.5 * (value + entry(j, i))
            for k in range(j):
                value = value - low[i, k] * low[j, k]
            if i == j:
                guess = lax.rsqrt(value)
                inverse[j] = guess * (1.5 - 0.5 * value * guess * guess)
            else:
                low[i, j] = value * inverse[j]

    def solve(sources):
        def part(k):
            rows = pl.ds(8 * k, 8)
            done = []
            for i, (ref, p) in enumerate(sources):
                value = ref[p, rows, :]
                for j in range(i):
                    value = value - low[i, j] * done[j]
                value = value * inverse[i]
                done.append(value)
                if i >= len(sources) - HALF:
                    factor_here[i - len(sources) + HALF, rows, :] = value

        unrolled(ROWS // 8, part)

    @pl.when(half == 0)
    def _():
        solve([(images, p) for p in range(HALF)])

    @pl.when(half == 1)
    def _():
        solve([(other_images, p) for p in range(HALF)] + [(images, p) for p in range(HALF)])

    factor_copy = pltpu.make_async_copy(factor_here, factor, sems.at[2])
    factor_copy.start()
    images_copy.wait()
    gram_copy.wait()
    factor_copy.wait()


def body(probes, velocity, eta, friction, noise, ice):
    nx_devices, ny_devices = lax.axis_size("gx"), lax.axis_size("gy")
    vmem = lambda *shape: pltpu.VMEM(shape, F32)
    dma = lambda count: pltpu.SemaphoreType.DMA((count,))
    grid = (BI, BJ, 8, 128)
    padded = (BI + 2, BJ + 2, 8, 128)
    whole = pl.BlockSpec(memory_space=pltpu.VMEM)
    tile = jax.ShapeDtypeStruct((HALF, ROWS, COLS), F32)
    images, other_images, sums = pl.pallas_call(
        functools.partial(main_kernel, nx_devices, ny_devices),
        out_shape=(tile, tile, jax.ShapeDtypeStruct((8, 128), F32)),
        in_specs=[pl.BlockSpec(memory_space=pl.ANY)] * 6,
        out_specs=(whole, whole, whole),
        scratch_shapes=[
            vmem(8, EXT + ROOM, 128), vmem(EXT, 128), vmem(EXT, 128), vmem(ROWS, 128), vmem(ROWS, 128),
            vmem(ROWS + 2 * ETA_HALO + ROOM, 128), vmem(3, 16, 128), vmem(3, 16, 128), vmem(16, 128), vmem(16, 128),
            vmem(2, ROWS, COLS), vmem(ROWS, COLS), pltpu.VMEM((ROWS, COLS), jnp.int32),
            vmem(2, EXT + ROOM, 128), vmem(ROWS + 2 * ETA_HALO + ROOM, 128),
            vmem(5, *grid), vmem(*padded), vmem(16, *grid), vmem(2, *grid), vmem(2, *grid),
            vmem(2, *padded), vmem(2, *padded),
            vmem(HALF, EXT + ROOM, 128), vmem(HALF, ROWS, COLS), vmem(1, 1, 128), vmem(2 * nx_devices * ny_devices, 1, 128),
            dma(6), dma(8), dma(8), dma(8), dma(8), dma(2), dma(2),
            pltpu.SemaphoreType.DMA, pltpu.SemaphoreType.DMA,
            pltpu.SemaphoreType.REGULAR((4,)),
        ],
        compiler_params=pltpu.CompilerParams(
            collective_id=0, has_side_effects=True, vmem_limit_bytes=32 * 1024 * 1024
        ),
    )(*[pltpu.with_memory_space_constraint(x, pltpu.HBM) for x in (probes, velocity, eta, friction, noise, ice)])
    square = (2 * HALF, 2 * HALF)
    return pl.pallas_call(
        last_kernel,
        out_shape=(tile, tile, jax.ShapeDtypeStruct(square, F32)),
        in_specs=[whole, whole, whole],
        out_specs=(pl.BlockSpec(memory_space=pl.ANY),) * 3,
        scratch_shapes=[vmem(HALF, ROWS, COLS), vmem(*square), dma(3)],
        compiler_params=pltpu.CompilerParams(vmem_limit_bytes=16 * 1024 * 1024),
    )(sums, images, other_images)


def solution(mesh):
    in_specs = (
        P("probe", "gx", "gy"),
        P(None, "gx", "gy"),
        P("gx", "gy"),
        P("gx", "gy"),
        P("gx", "gy"),
        P("gx", "gy"),
    )
    out_specs = (P("probe", "gx", "gy"), P("probe", "gx", "gy"), P())
    return jax.shard_map(body, mesh=mesh, in_specs=in_specs, out_specs=out_specs, check_vma=False)
```

```python
import functools

import jax
import jax.numpy as jnp
import numpy as np
from jax import lax
from jax.experimental import pallas as pl
from jax.experimental.pallas import tpu as pltpu
from jax.sharding import PartitionSpec as P

SWEEPS = 9
OMEGA = 0.6
DRAG = 0.05
PRIOR = 0.05

HALF = 4
ROWS, COLS = 64, 128
HALO = 2 * (SWEEPS - 1)
BI, BJ = (ROWS + 2 * HALO) // 8, (COLS + 2 * HALO) // 32
EXT = ROWS + 2 * HALO
ROOM = 16
ETA_HALO = 24
MESH = pl.DeviceIdType.MESH
F32 = jnp.float32
SERIES = np.polynomial.Polynomial([0.0])
for power in range(SWEEPS):
    SERIES = SERIES + np.polynomial.Polynomial([1.0 - OMEGA, OMEGA]) ** power
SERIES = [float(a) for a in SERIES.coef]
AROUND = ((-1, 0), (1, 0), (0, -1), (0, 1), (-1, -1), (-1, 1), (1, -1), (1, 1))


def lanes():
    return lax.broadcasted_iota(jnp.int32, (8, 128), 1)


def sublanes():
    return lax.broadcasted_iota(jnp.int32, (8, 128), 0)


def turn(x, shift, axis):
    shift = shift % x.shape[axis]
    return pltpu.roll(x, shift, axis) if shift else x


def pick(x, index):
    return jnp.take_along_axis(x, index, axis=1, mode="promise_in_bounds")


def unrolled(count, body, start=0):
    def step(i, carry):
        body(i)
        return carry

    lax.fori_loop(start, count, step, 0, unroll=True)


def ends_first(body):
    body(0)
    body(BI - 1)
    unrolled(BI - 1, body, 1)


def pack_strips(ext, eta, left, right, eta_left, eta_right):
    lane = lax.broadcasted_iota(jnp.int32, (ROWS, COLS), 1)
    for f in range(8):
        own = ext[f, HALO : HALO + ROWS, :]
        here = (lane >= 16 * f) & (lane < 16 * f + 16)
        first, last = turn(own, 16 * f, 1), turn(own, 16 * f + 16, 1)
        left[...] = first if f == 0 else jnp.where(here, first, left[...])
        right[...] = last if f == 0 else jnp.where(here, last, right[...])
    lane = lax.broadcasted_iota(jnp.int32, (16, COLS), 1)
    first = last = None
    for g in range(4):
        own = eta[ETA_HALO + 16 * g : ETA_HALO + 16 * g + 16, :]
        here = (lane >= 32 * g) & (lane < 32 * g + 32)
        a, b = turn(own, 32 * g, 1), turn(own, 32 * g + 32, 1)
        first = a if g == 0 else jnp.where(here, a, first)
        last = b if g == 0 else jnp.where(here, b, last)
    eta_left[...] = first
    eta_right[...] = last


def places(j):
    col = BJ * (lanes() & 31) + j - HALO
    return col, jnp.clip(col, 0, COLS - 1), (col < 0) | (col >= COLS)


def relayout_own(ext, eta, spread, eta_spread):
    group = lanes() >> 5

    def fields(i):
        rows = pl.ds(i, 8, stride=BI)
        own = [ext[f, rows, :] for f in range(8)]
        for j in range(BJ):
            _, at, _ = places(j)
            value = pick(own[HALF - 1], at)
            for p in range(HALF - 2, -1, -1):
                value = jnp.where(group == p, pick(own[p], at), value)
            spread[0, i, j] = value
            for f in range(4):
                spread[1 + f, i, j] = pick(own[4 + f], at)

    unrolled(BI, fields)

    def viscosity(i):
        own = eta[pl.ds(i + ETA_HALO - HALO - 1, 8, stride=BI), :]
        for j in range(-1, BJ + 1):
            eta_spread[i, j + 1] = pick(own, places(j)[1])

    unrolled(BI + 2, viscosity)


def relayout_sides(west, east, eta_west, eta_east, side, eta_side, spread, eta_spread):
    lane = lanes()
    group = lane >> 5
    wide = lax.broadcasted_iota(jnp.int32, (EXT, COLS), 1)
    w, e = west[...], east[...]
    side[0, 0:EXT, :] = jnp.where(wide < 64, w, turn(e, 64, 1))
    side[1, 0:EXT, :] = jnp.where(wide < 64, turn(w, 64, 1), e)
    for k in range(14):
        own_row = 8 * k - ETA_HALO
        slot = 0 if own_row < 0 else (1 if own_row < ROWS else 2)
        row = own_row - ROWS * (slot - 1)
        g, r = row // 16, row % 16
        a = turn(eta_west[slot, r : r + 8, :], -32 * g, 1)
        b = turn(eta_east[slot, r : r + 8, :], 32 - 32 * g, 1)
        eta_side[8 * k : 8 * k + 8, :] = jnp.where(lane < 32, a, b)

    def viscosity(i):
        beside = eta_side[pl.ds(i + ETA_HALO - HALO - 1, 8, stride=BI), :]
        for j in range(-1, BJ + 1):
            col, _, outside = places(j)
            at = jnp.where(outside, jnp.where(col < 0, col + 32, col - COLS + 32), 0)
            eta_spread[i, j + 1] = jnp.where(outside, pick(beside, at), eta_spread[i, j + 1])

    unrolled(BI + 2, viscosity)

    def fields(i):
        rows = pl.ds(i, 8, stride=BI)
        low, high = side[0, rows, :], side[1, rows, :]
        for j in range(BJ):
            col, _, outside = places(j)
            at = jnp.where(outside, jnp.where(col < 0, col + HALO, col - COLS + 64), 0)
            spread[0, i, j] = jnp.where(outside, pick(low, at + 16 * group), spread[0, i, j])
            for f in range(4):
                spread[1 + f, i, j] = jnp.where(outside, pick(high, at + 16 * f), spread[1 + f, i, j])

    unrolled(BI, fields)


def store_state(state, c, i, values):
    values = [turn(values[BJ - 1], 1, 1)] + values + [turn(values[0], -1, 1)]
    for j, value in enumerate(values):
        state[c, i + 1, j] = value
    if isinstance(i, int):
        for j, value in enumerate(values):
            if i == 0:
                state[c, BI + 1, j] = turn(value, -1, 0)
            else:
                state[c, 0, j] = turn(value, 1, 0)


def recip(x):
    y = pl.reciprocal(x, approx=True)
    y = y * (2.0 - x * y)
    return y * (2.0 - x * y)


def coefficients(spread, eta_spread, coef, weight, source, state, gx, gy, nx, ny):
    lane, sub = lanes(), sublanes()

    def row(i):
        r = gx * ROWS - HALO + BI * sub + i
        row_in = (r >= 0) & (r < nx)
        first, second = [], []
        for j in range(BJ):
            c = gy * COLS - HALO + BJ * (lane & 31) + j
            inside = row_in & (c >= 0) & (c < ny)
            m = eta_spread[i + 1, j + 1]
            e, w = eta_spread[i + 2, j + 1], eta_spread[i, j + 1]
            n, s = eta_spread[i + 1, j + 2], eta_spread[i + 1, j]
            react = spread[3, i, j] + DRAG
            me, mw, mn, ms = m + e, m + w, m + n, m + s
            along, across = me + mw, mn + ms
            w1 = jnp.where(inside, recip(2.0 * along + 0.5 * across + react), 0.0)
            w2 = jnp.where(inside, recip(0.5 * along + 2.0 * across + react), 0.0)
            a1, b1, q1 = 2.0 * w1, 0.5 * w1, 0.25 * w1
            a2, b2, q2 = 2.0 * w2, 0.5 * w2, 0.25 * w2
            coef[0, i, j] = a1 * me
            coef[1, i, j] = a1 * mw
            coef[2, i, j] = b1 * mn
            coef[3, i, j] = b1 * ms
            be, bw, qn, qs = b1 * e, b1 * w, q1 * n, q1 * s
            coef[4, i, j] = be + qn
            coef[5, i, j] = be + qs
            coef[6, i, j] = bw + qn
            coef[7, i, j] = bw + qs
            coef[8, i, j] = b2 * me
            coef[9, i, j] = b2 * mw
            coef[10, i, j] = a2 * mn
            coef[11, i, j] = a2 * ms
            bn, bs, qe, qw = b2 * n, b2 * s, q2 * e, q2 * w
            coef[12, i, j] = bn + qe
            coef[13, i, j] = bs + qe
            coef[14, i, j] = bn + qw
            coef[15, i, j] = bs + qw
            w1, w2 = OMEGA * w1, OMEGA * w2
            noise = spread[4, i, j]
            weight[0, i, j] = w1 * noise
            weight[1, i, j] = w2 * noise
            probe = spread[0, i, j]
            f1, f2 = w1 * (spread[1, i, j] * probe), w2 * (spread[2, i, j] * probe)
            source[0, i, j] = f1
            source[1, i, j] = f2
            first.append(SERIES[-1] * f1)
            second.append(SERIES[-1] * f2)
        store_state(state, 0, i, first)
        store_state(state, 1, i, second)

    ends_first(row)


def sweep(old, new, coef, source, factor):
    def row(i):
        first, second = [], []
        for j in range(BJ):

            def at(c, di, dj):
                return old[c, i + 1 + di, j + 1 + dj]

            k = [coef[n, i, j] for n in range(16)]
            first.append(
                factor * source[0, i, j]
                + (k[0] * at(0, 1, 0) + k[1] * at(0, -1, 0))
                + (k[2] * at(0, 0, 1) + k[3] * at(0, 0, -1))
                + (k[4] * at(1, 1, 1) - k[5] * at(1, 1, -1))
                + (k[7] * at(1, -1, -1) - k[6] * at(1, -1, 1))
            )
            second.append(
                factor * source[1, i, j]
                + (k[8] * at(1, 1, 0) + k[9] * at(1, -1, 0))
                + (k[10] * at(1, 0, 1) + k[11] * at(1, 0, -1))
                + (k[12] * at(0, 1, 1) - k[13] * at(0, 1, -1))
                + (k[15] * at(0, -1, -1) - k[14] * at(0, -1, 1))
            )
        store_state(new, 0, i, first)
        store_state(new, 1, i, second)

    ends_first(row)


def relax_twice(state_a, state_b, coef, source, between):

    def step(k, carry):
        for n in range(SWEEPS - 1):
            factor = SERIES[SWEEPS - 2 - n]
            old, new = (state_a, state_b) if n % 2 == 0 else (state_b, state_a)
            sweep(old, new, coef, source, factor)

        @pl.when(k == 0)
        def _():
            between()

        return carry

    lax.fori_loop(0, 2, step, 0)


def next_source(state, weight, source):
    def row(i):
        for c in range(2):
            values = [weight[c, i, j] * state[c, i + 1, j + 1] for j in range(BJ)]
            for j in range(BJ):
                source[c, i, j] = values[j]
            store_state(state, c, i, [SERIES[-1] * value for value in values])

    ends_first(row)


def gather_images(state, spread, natural):
    lane = lanes()
    place = lane + HALO
    block = (place * 205) >> 10
    rest = place - BJ * block

    def row(i):
        values = [
            spread[1, i, j] * state[0, i + 1, j + 1]
            + spread[2, i, j] * state[1, i + 1, j + 1]
            + PRIOR * spread[0, i, j]
            for j in range(BJ)
        ]
        for p in range(HALF):
            out = pick(values[0], block + 32 * p)
            for j in range(1, BJ):
                out = jnp.where(rest == j, pick(values[j], block + 32 * p), out)
            natural[p, pl.ds(i, 8, stride=BI), :] = out

    unrolled(BI, row)


def products(lefts, right, right_row):
    count = 16 * len(lefts)

    def add(k, totals):
        a = [left[p, pl.ds(row + 8 * k, 8), :] for left, row in lefts for p in range(HALF)]
        b = [right[p, pl.ds(right_row + 8 * k, 8), :] for p in range(HALF)]
        return tuple(t + a[n // 4] * b[n % 4] for n, t in enumerate(totals))

    zero = jnp.zeros((8, 128), F32)
    totals = lax.fori_loop(0, ROWS // 8, add, (zero,) * count, unroll=True)
    sums = jnp.concatenate([jnp.sum(t, axis=0, keepdims=True) for t in totals], axis=0)
    sums = jnp.sum(sums, axis=1, keepdims=True)
    lane = lax.broadcasted_iota(jnp.int32, (count, 128), 1)
    row = lax.broadcasted_iota(jnp.int32, (count, 128), 0)
    return jnp.sum(jnp.where(lane == row, sums, 0.0), axis=0, keepdims=True)


def main_kernel(
    nx_devices, ny_devices,
    probes, velocity, eta_in, friction, noise, ice,
    images, other_images, gram,
    ext, west, east, left, right, eta, eta_west, eta_east, eta_left, eta_right,
    vel, fric, mask, side, eta_side, spread, eta_spread, coef, weight, source, state_a, state_b,
    natural, other_probes, message, inbox,
    in_sem, halo_send, halo_recv, eta_send, eta_recv, pair_send, pair_recv,
    sum_send, sum_recv, heard,
):
    half, gx, gy = lax.axis_index("probe"), lax.axis_index("gx"), lax.axis_index("gy")
    own_rows = slice(HALO, HALO + ROWS)

    loads = [
        pltpu.make_async_copy(velocity, vel, in_sem.at[0]),
        pltpu.make_async_copy(friction, fric, in_sem.at[1]),
        pltpu.make_async_copy(ice, mask, in_sem.at[2]),
        pltpu.make_async_copy(probes, ext.at[0:HALF, own_rows, :], in_sem.at[3]),
        pltpu.make_async_copy(noise, ext.at[7, own_rows, :], in_sem.at[4]),
        pltpu.make_async_copy(eta_in, eta.at[ETA_HALO : ETA_HALO + ROWS, :], in_sem.at[5]),
    ]
    for load in loads:
        load.start()

    def blank(ref):
        ref[...] = jnp.zeros(ref.shape, F32)

    @pl.when(gx == 0)
    def _():
        blank(ext.at[:, 0:HALO, :])
        blank(eta.at[0:ETA_HALO, :])
        for ref in (west, east):
            blank(ref.at[0:HALO, :])
        for ref in (eta_west, eta_east):
            blank(ref.at[0])

    @pl.when(gx == nx_devices - 1)
    def _():
        blank(ext.at[:, HALO + ROWS : EXT, :])
        blank(eta.at[ETA_HALO + ROWS : 2 * ETA_HALO + ROWS, :])
        for ref in (west, east):
            blank(ref.at[HALO + ROWS : EXT, :])
        for ref in (eta_west, eta_east):
            blank(ref.at[2])

    @pl.when(gy == 0)
    def _():
        blank(west)
        blank(eta_west)

    @pl.when(gy == ny_devices - 1)
    def _():
        blank(east)
        blank(eta_east)

    def exists(dx, dy):
        x, y = gx + dx, gy + dy
        return (x >= 0) & (x < nx_devices) & (y >= 0) & (y < ny_devices)

    def away(dx, dy):
        return {"gx": lax.rem(gx + dx + nx_devices, nx_devices), "gy": lax.rem(gy + dy + ny_devices, ny_devices)}

    partner = {"probe": 1 - half}

    def signal(semaphore, to):
        pl.semaphore_signal(semaphore, inc=1, device_id=to, device_id_type=MESH)

    barrier = pltpu.get_barrier_semaphore()
    for dx, dy in AROUND:
        signal(barrier, away(dx, dy))
    signal(barrier, partner)

    relays = (AROUND, [(2 * dx, 2 * dy) for dx, dy in AROUND], [(-4, 0), (4, 0)], [])

    def relay(stage):
        for dx, dy in relays[stage]:
            signal(heard.at[stage], away(dx, dy))
        signal(heard.at[stage], partner)

    def hear(stage):
        pl.semaphore_wait(heard.at[stage], len(relays[stage]) + 1)

    for load in loads:
        load.wait()
    coupling = fric[...] * mask[...].astype(F32)
    ext[4, own_rows, :] = -coupling * vel[0]
    ext[5, own_rows, :] = -coupling * vel[1]
    ext[6, own_rows, :] = coupling
    pack_strips(ext, eta, left, right, eta_left, eta_right)

    pl.semaphore_wait(barrier, len(AROUND) + 1)

    def halo_copies(n):
        dx, dy = AROUND[n]
        to = {"gx": gx + dx, "gy": gy + dy}
        if dy == 0:
            src_row, dst_row = (ROWS, 0) if dx > 0 else (HALO, HALO + ROWS)
            main = (ext.at[:, src_row : src_row + HALO, :], ext.at[:, dst_row : dst_row + HALO, :])
            src_row, dst_row = (ROWS, 0) if dx > 0 else (ETA_HALO, ETA_HALO + ROWS)
            more = (eta.at[src_row : src_row + ETA_HALO, :], eta.at[dst_row : dst_row + ETA_HALO, :])
        else:
            strip, landing = (right, west) if dy > 0 else (left, east)
            src_row, dst_row, count = {0: (0, HALO, ROWS), 1: (ROWS - HALO, 0, HALO), -1: (0, HALO + ROWS, HALO)}[dx]
            main = (strip.at[src_row : src_row + count, :], landing.at[dst_row : dst_row + count, :])
            strip, landing = (eta_right, eta_west) if dy > 0 else (eta_left, eta_east)
            more = (strip, landing.at[1 - dx])
        return [
            pltpu.make_async_remote_copy(
                src_ref=src, dst_ref=dst, send_sem=sends.at[n], recv_sem=recvs.at[n], device_id=to, device_id_type=MESH
            )
            for (src, dst), sends, recvs in ((main, halo_send, halo_recv), (more, eta_send, eta_recv))
        ]

    for n, (dx, dy) in reversed(list(enumerate(AROUND))):

        @pl.when(exists(dx, dy))
        def _():
            for copy in halo_copies(n):
                copy.start()

    relay(0)

    probe_copy = pltpu.make_async_remote_copy(
        src_ref=ext.at[0:HALF, own_rows, :], dst_ref=other_probes,
        send_sem=pair_send.at[0], recv_sem=pair_recv.at[0], device_id={"probe": 1 - half}, device_id_type=MESH,
    )
    image_copy = pltpu.make_async_remote_copy(
        src_ref=natural.at[:, own_rows, :], dst_ref=other_images,
        send_sem=pair_send.at[1], recv_sem=pair_recv.at[1], device_id={"probe": 1 - half}, device_id_type=MESH,
    )

    def await_halos(directions):
        for n in directions:
            dx, dy = AROUND[n]

            @pl.when(exists(-dx, -dy))
            def _():
                for copy in halo_copies(n):
                    copy.wait_recv()

    await_halos((0, 1))
    relayout_own(ext, eta, spread, eta_spread)
    hear(0)
    relay(1)
    await_halos(range(2, 8))

    @pl.when(half == 1)
    def _():
        probe_copy.start()

    relayout_sides(west, east, eta_west, eta_east, side, eta_side, spread, eta_spread)
    coefficients(
        spread, eta_spread, coef, weight, source, state_a, gx, gy, nx_devices * ROWS, ny_devices * COLS
    )
    hear(1)
    relay(2)

    def between():
        next_source(state_a, weight, source)
        hear(2)
        relay(3)

    relax_twice(state_a, state_b, coef, source, between)
    gather_images(state_a, spread, natural)

    @pl.when(half == 0)
    def _():
        image_copy.start()


    @pl.when(half == 0)
    def _():
        probe_copy.wait_recv()
        message[0] = products([(ext, HALO), (other_probes, 0)], natural, HALO)

    @pl.when(half == 1)
    def _():
        message[0] = turn(products([(ext, HALO)], natural, HALO), 32, 1)

    hear(3)

    me = (gx * ny_devices + gy) * 2 + half
    everyone = 2 * nx_devices * ny_devices

    def sum_copy(dx, dy, dp, to_all):
        to = {
            "gx": lax.rem(gx + dx, nx_devices),
            "gy": lax.rem(gy + dy, ny_devices),
            "probe": lax.rem(half + dp, 2),
        }
        rows = everyone - 1 if to_all else 1
        src = inbox.at[0:rows] if to_all else message
        dst = inbox.at[0:rows] if to_all else inbox.at[pl.ds(me, 1)]
        return pltpu.make_async_remote_copy(
            src_ref=src, dst_ref=dst, send_sem=sum_send, recv_sem=sum_recv, device_id=to, device_id_type=MESH
        )

    y_order = (4, 3, 5, 2, 6, 1, 7, 0)

    def send_sums(k, carry):
        step = lax.div(k + 1, 2)
        dx = lax.rem(nx_devices // 2 + nx_devices + jnp.where(lax.rem(k, 2) == 0, step, -step), nx_devices)
        for dy in y_order:
            for dp in (1, 0):
                if dy == 0 and dp == 0:

                    @pl.when(dx != 0)
                    def _():
                        sum_copy(dx, dy, dp, False).start()
                else:
                    sum_copy(dx, dy, dp, False).start()
        return carry

    lax.fori_loop(0, nx_devices, send_sums, 0)
    inbox[pl.ds(me, 1)] = message[...]
    images[...] = natural[:, own_rows, :]
    all_sums = sum_copy(1, 0, 0, True)
    all_sums.wait_recv()
    total = jnp.sum(jnp.sum(inbox[...].reshape(everyone // 8, 8, 128), axis=0), axis=0, keepdims=True)
    gram[...] = jnp.broadcast_to(total * (1.0 / (nx_devices * ROWS * ny_devices * COLS)), (8, 128))

    for n, (dx, dy) in enumerate(AROUND):

        @pl.when(exists(dx, dy))
        def _():
            for copy in halo_copies(n):
                copy.wait_send()

    all_sums.wait_send()

    @pl.when(half == 0)
    def _():
        image_copy.wait_send()

    @pl.when(half == 1)
    def _():
        probe_copy.wait_send()
        image_copy.wait_recv()


def last_kernel(sums, images, other_images, images_out, factor, gram, factor_here, gram_here, sems):
    half = lax.axis_index("probe")
    images_copy = pltpu.make_async_copy(images, images_out, sems.at[0])
    images_copy.start()

    lane, sub = lanes(), sublanes()
    low_row, low_col = sub < HALF, lane < HALF
    a, b = sub & (HALF - 1), lane & (HALF - 1)
    at = jnp.where(low_row == low_col, HALF * a + b, jnp.where(low_col, HALF * a + b, HALF * b + a))
    at = at + jnp.where(low_row == low_col, jnp.where(low_row, 0, 2 * HALF * HALF), HALF * HALF)
    row = sums[...]
    full = pick(row, jnp.where(lane < 2 * HALF, at, 0))
    gram_here[...] = full[:, : 2 * HALF]
    gram_copy = pltpu.make_async_copy(gram_here, gram, sems.at[1])
    gram_copy.start()

    def entry(i, j):
        k = HALF * (i % HALF) + j % HALF
        if (i < HALF) == (j < HALF):
            return jnp.broadcast_to(row[:, (k if i < HALF else k + 32) :][:, :1], (8, 128))
        return jnp.broadcast_to(row[:, k + 16 :][:, :1], (8, 128))

    count = 2 * HALF
    low, inverse = {}, {}
    for j in range(count):
        for i in range(j, count):
            value = entry(i, j)
            if i != j and (i < HALF) == (j < HALF):
                value = 0.5 * (value + entry(j, i))
            for k in range(j):
                value = value - low[i, k] * low[j, k]
            if i == j:
                guess = lax.rsqrt(value)
                inverse[j] = guess * (1.5 - 0.5 * value * guess * guess)
            else:
                low[i, j] = value * inverse[j]

    def solve(sources):
        def part(k):
            rows = pl.ds(8 * k, 8)
            done = []
            for i, (ref, p) in enumerate(sources):
                value = ref[p, rows, :]
                for j in range(i):
                    value = value - low[i, j] * done[j]
                value = value * inverse[i]
                done.append(value)
                if i >= len(sources) - HALF:
                    factor_here[i - len(sources) + HALF, rows, :] = value

        unrolled(ROWS // 8, part)

    @pl.when(half == 0)
    def _():
        solve([(images, p) for p in range(HALF)])

    @pl.when(half == 1)
    def _():
        solve([(other_images, p) for p in range(HALF)] + [(images, p) for p in range(HALF)])

    factor_copy = pltpu.make_async_copy(factor_here, factor, sems.at[2])
    factor_copy.start()
    images_copy.wait()
    gram_copy.wait()
    factor_copy.wait()


def body(probes, velocity, eta, friction, noise, ice):
    nx_devices, ny_devices = lax.axis_size("gx"), lax.axis_size("gy")
    vmem = lambda *shape: pltpu.VMEM(shape, F32)
    dma = lambda count: pltpu.SemaphoreType.DMA((count,))
    grid = (BI, BJ, 8, 128)
    padded = (BI + 2, BJ + 2, 8, 128)
    whole = pl.BlockSpec(memory_space=pltpu.VMEM)
    tile = jax.ShapeDtypeStruct((HALF, ROWS, COLS), F32)
    images, other_images, sums = pl.pallas_call(
        functools.partial(main_kernel, nx_devices, ny_devices),
        out_shape=(tile, tile, jax.ShapeDtypeStruct((8, 128), F32)),
        in_specs=[pl.BlockSpec(memory_space=pl.ANY)] * 6,
        out_specs=(whole, whole, whole),
        scratch_shapes=[
            vmem(8, EXT + ROOM, 128), vmem(EXT, 128), vmem(EXT, 128), vmem(ROWS, 128), vmem(ROWS, 128),
            vmem(ROWS + 2 * ETA_HALO + ROOM, 128), vmem(3, 16, 128), vmem(3, 16, 128), vmem(16, 128), vmem(16, 128),
            vmem(2, ROWS, COLS), vmem(ROWS, COLS), pltpu.VMEM((ROWS, COLS), jnp.int32),
            vmem(2, EXT + ROOM, 128), vmem(ROWS + 2 * ETA_HALO + ROOM, 128),
            vmem(5, *grid), vmem(*padded), vmem(16, *grid), vmem(2, *grid), vmem(2, *grid),
            vmem(2, *padded), vmem(2, *padded),
            vmem(HALF, EXT + ROOM, 128), vmem(HALF, ROWS, COLS), vmem(1, 1, 128), vmem(2 * nx_devices * ny_devices, 1, 128),
            dma(6), dma(8), dma(8), dma(8), dma(8), dma(2), dma(2),
            pltpu.SemaphoreType.DMA, pltpu.SemaphoreType.DMA,
            pltpu.SemaphoreType.REGULAR((4,)),
        ],
        compiler_params=pltpu.CompilerParams(
            collective_id=0, has_side_effects=True, vmem_limit_bytes=32 * 1024 * 1024
        ),
    )(*[pltpu.with_memory_space_constraint(x, pltpu.HBM) for x in (probes, velocity, eta, friction, noise, ice)])
    square = (2 * HALF, 2 * HALF)
    return pl.pallas_call(
        last_kernel,
        out_shape=(tile, tile, jax.ShapeDtypeStruct(square, F32)),
        in_specs=[whole, whole, whole],
        out_specs=(pl.BlockSpec(memory_space=pl.ANY),) * 3,
        scratch_shapes=[vmem(HALF, ROWS, COLS), vmem(*square), dma(3)],
        compiler_params=pltpu.CompilerParams(vmem_limit_bytes=16 * 1024 * 1024),
    )(sums, images, other_images)


def solution(mesh):
    in_specs = (
        P("probe", "gx", "gy"),
        P(None, "gx", "gy"),
        P("gx", "gy"),
        P("gx", "gy"),
        P("gx", "gy"),
        P("gx", "gy"),
    )
    out_specs = (P("probe", "gx", "gy"), P("probe", "gx", "gy"), P())
    return jax.shard_map(body, mesh=mesh, in_specs=in_specs, out_specs=out_specs, check_vma=False)
```
